512 devices in a mesh: aa: 32 (over z, core), ba: 16 (over x, y).
Axes of the slice: x: 4, y: 4, z: 16, core: 2. Of those that a mesh axis runs over, the one named last changes fastest.
Arguments:
- legendre: bfloat16 [640, 32, 16, 1, 1281], P('aa', None, 'ba'), may hold values from -0.15625 to 0.15625
- spectral: bfloat16 [640, 1281, 2, 64], P('aa', None, None, 'ba'), may hold values from -0.25 to 0.25
- slot_pairs: int32 [640], replicated, may hold values from 0 to 639, each once
- lat_shift: int32 [512, 5120], P('aa', 'ba'), may hold values from -1 to 1
- lon_shift: int32 [512, 5120], P('aa', 'ba'), may hold values from -8 to 8
Outputs:
- departed: bfloat16 [512, 64, 5120], P('aa', None, 'ba')
The draws below stay inside these ranges and needn't reach their ends.
Inputs may be any that keep to these rules, and one draw needn't show every extreme that they name: `slot_pairs`: each pair index appears in exactly one slot.
All inputs are finite; a program needn't handle non-finite values.
Results may differ from the reference program's by a relative error of at most 0.0059.
Values may be sent and summed in bfloat16 or wider, within the bound.
No kernel may reach another device: no remote copies, remote signals or barrier semaphores. Data moves between devices by JAX's collectives and lax.ppermute only.
A program may use at most 64 MiB of HBM per device.

```python
import math
import jax
import jax.numpy as jnp
from jax import lax

WAVES = 1280
NLON = 5120
ROWS = 1
HMAX = 8
FL = 64
NPAIR = 640
KPACK = 1281
LATS = 512
N_AA = 32
N_BA = 16


def plant(entries, key, smallest, high):
    dims = entries.shape
    place = [jax.random.randint(jax.random.fold_in(key, axis), (), 0, dims[axis]) for axis in range(len(dims))]
    entries = entries.at[tuple(place)].set(smallest)
    longest = dims.index(max(dims))
    place[longest] = (place[longest] + 1) % dims[longest]
    return entries.at[tuple(place)].set(high)


def block_scale(own_key, shape, shards, smallest, largest):
    gain = 1.0
    for dim, shards_of in shards:
        steps = jax.random.uniform(jax.random.fold_in(jax.random.fold_in(own_key, 6), dim), (shards_of,), jnp.float32, smallest / len(shards), largest / len(shards))
        gain = gain * jnp.repeat(jnp.exp(steps), shape[dim] // shards_of).reshape((-1,) + (1,) * (len(shape) - 1 - dim))
    return gain


def gaussian(key, dims, spread, reach, cuts=(), kind=jnp.bfloat16):
    entries = spread * jax.random.normal(key, dims, jnp.float32)
    if cuts:
        entries = entries * block_scale(key, dims, cuts, -0.22, 0.18)
    return jnp.clip(entries, -reach, reach).astype(kind)


def setup_inputs(seed: int = 0) -> dict:
    key_of = jax.random.split(jax.random.key(seed), 6)
    legendre = gaussian(key_of[0], (NPAIR, N_AA, N_BA, ROWS, KPACK), KPACK ** -0.5, 0.15625, ((0, 32), (2, 16)))
    spectral = gaussian(key_of[1], (NPAIR, KPACK, 2, FL), ((2.0 / WAVES) ** 0.5), 0.25, ((0, 32), (3, 16)))
    slot_pairs = jax.random.permutation(key_of[2], NPAIR).astype(jnp.int32)
    lat_shift = plant(jax.random.randint(key_of[3], (LATS, NLON), -1, 2), jax.random.fold_in(key_of[3], 1), -1, 1).astype(jnp.int32)
    lon_shift = plant(jax.random.randint(key_of[4], (LATS, NLON), -HMAX, HMAX + 1), jax.random.fold_in(key_of[4], 1), -HMAX, HMAX).astype(jnp.int32)
    return dict(legendre=legendre, spectral=spectral, slot_pairs=slot_pairs, lat_shift=lat_shift, lon_shift=lon_shift)


STENCIL = (-0.0625, 0.5625, 0.5625, -0.0625)

def pair_masks(pairs):
    column = jnp.arange(KPACK, dtype=jnp.int32)[None, :]
    lower = column < (WAVES - pairs)[:, None]
    return jnp.stack([lower, jnp.logical_not(lower)], axis=-1).astype(jnp.bfloat16)

def fourier_table(slot_pairs, first_lon, lon_count):
    waves_of = jnp.stack([slot_pairs, WAVES - 1 - slot_pairs], axis=1).astype(jnp.int32)
    lon_ids = first_lon + jnp.arange(lon_count, dtype=jnp.int32)
    phases = waves_of[:, :, None] * lon_ids[None, None, :] % NLON
    angles = phases.astype(jnp.float32) * (2.0 * math.pi / NLON)
    factor = 1.0 / math.sqrt(WAVES)
    stacked = jnp.stack([jnp.cos(angles) * factor, -jnp.sin(angles) * factor], axis=2)
    return stacked.reshape(2 * WAVES, lon_count).astype(jnp.bfloat16)

def synthesize(coefficients, slot_pairs):
    block_width = 512 if NLON % 512 == 0 else NLON
    count_blocks = NLON // block_width

    def one_block(block_id):
        synth_table = fourier_table(slot_pairs, block_id * block_width, block_width)
        return jnp.dot(coefficients, synth_table, preferred_element_type=jnp.float32).astype(jnp.bfloat16)
    pieces = lax.map(one_block, jnp.arange(count_blocks, dtype=jnp.int32))
    return pieces.transpose(1, 0, 2).reshape(coefficients.shape[0], NLON)

def depart(padded, lat_shift, lon_shift, halo_width):
    count_rows, columns = lat_shift.shape
    fields = padded.shape[1]
    span = padded.shape[2]
    flat_field = padded.transpose(1, 0, 2).reshape(fields, -1)
    row_ids = jnp.arange(count_rows, dtype=jnp.int32)[:, None]
    col_ids = jnp.arange(columns, dtype=jnp.int32)[None, :]
    start_ids = ((row_ids + 1 + lat_shift) * span + col_ids + halo_width - 1 + lon_shift).reshape(-1)
    summed = jnp.zeros((fields, count_rows * columns), jnp.float32)
    for position, weight in enumerate(STENCIL):
        summed = summed + weight * jnp.take(flat_field, start_ids + position, axis=1).astype(jnp.float32)
    return summed.reshape(fields, count_rows, columns).transpose(1, 0, 2).astype(jnp.bfloat16)

def reference(legendre, spectral, slot_pairs, lat_shift, lon_shift):
    leg_all = legendre.reshape(NPAIR, LATS, KPACK)
    selected = spectral[:, :, None, :, :] * pair_masks(slot_pairs)[:, :, :, None, None]
    right_side = selected.reshape(NPAIR, KPACK, 4 * FL)

    def one_pair(items):
        leg_one, right_one = items
        return jnp.dot(leg_one, right_one, preferred_element_type=jnp.float32).astype(jnp.bfloat16)
    fourier_coef = lax.map(one_pair, (leg_all, right_side))
    coefficients = fourier_coef.reshape(NPAIR, LATS, 2, 2, FL).transpose(1, 4, 0, 2, 3).reshape(LATS * FL, 2 * WAVES)
    grid = synthesize(coefficients, slot_pairs).reshape(LATS, FL, NLON)
    halo_width = HMAX + 2
    padded = jnp.pad(grid, ((1, 1), (0, 0), (0, 0)))
    padded = jnp.concatenate([padded[:, :, NLON - halo_width:], padded, padded[:, :, :halo_width]], axis=2)
    return depart(padded, lat_shift, lon_shift, halo_width)
```

```python
import math

import jax
import jax.numpy as jnp
import numpy as np
from jax import lax
from jax.experimental import pallas as pl
from jax.experimental.pallas import tpu as pltpu
from jax.sharding import PartitionSpec as P

WAVES = 1280
NLON = 5120
FL = 64
KPACK = 1281
KPAD = 1408
N_AA = 32
N_BA = 16
PAIRS = 20
HALO = 32
QUARTER = NLON // 4
BLOCK = NLON // N_BA
WINDOW = BLOCK + 2 * HALO
BF16 = jnp.bfloat16
F32 = jnp.float32
NT = (((1,), (1,)), ((), ()))
FAR = -1000.0


def params(mib):
    return pltpu.CompilerParams(vmem_limit_bytes=mib * 1024 * 1024)


def whole(count):
    return [pl.BlockSpec(memory_space=pltpu.VMEM)] * count


def wave_order():
    pairs = np.arange(WAVES // 2)
    return np.concatenate([pairs, WAVES - 1 - pairs])


def window_table():
    starts = np.arange(4)[:, None] * BLOCK - HALO
    lons = (starts + np.arange(WINDOW)[None, :]).reshape(-1)
    phases = wave_order()[:, None] * lons[None, :] % NLON
    angles = phases.astype(np.float32) * np.float32(2.0 * math.pi / NLON)
    factor = np.float32(1.0 / math.sqrt(WAVES))
    table = np.concatenate([np.cos(angles) * factor, -np.sin(angles) * factor], axis=0)
    return table.astype(np.float32).astype(BF16)


def quarter_turns():
    turns = wave_order()[None, :] * np.arange(4)[:, None] % 4
    real = np.array([1, 0, -1, 0])[turns]
    imag = np.array([0, 1, 0, -1])[turns]
    return np.concatenate([real, imag], axis=0).astype(np.float32)


def field_order():
    c, b, f4 = np.meshgrid(np.arange(2), np.arange(N_BA), np.arange(4), indexing="ij")
    lanes = (b * 8 + c * 4 + f4).reshape(-1)
    return (lanes[:, None] == np.arange(128)[None, :]).astype(np.float32).astype(BF16)


def legendre_kernel(pairs_ref, rows_ref, out_ref):
    column = lax.broadcasted_iota(jnp.int32, (1, KPAD), 1)
    for which, (first, count, spec) in enumerate(((0, 32, 40), (32, 8, 48))):
        lower = (column < WAVES - pairs_ref[which]).astype(F32)
        values = rows_ref[:, spec : spec + 8, :].reshape(128, KPAD)
        right = jnp.concatenate(
            [values * lower.astype(BF16), values * (1.0 - lower).astype(BF16)], axis=0
        )
        left = rows_ref[:, first : first + count, :].reshape(N_BA * count, KPAD)
        out = lax.dot_general(left, right, NT, preferred_element_type=F32).astype(BF16)
        out_ref[:, first : first + count, :] = out.reshape(N_BA, count, 256)


def synthesis_kernel(slots_ref, turns_ref, fields_ref, coef_ref, table_ref, out_ref, left_ref):
    rows = coef_ref[...].reshape(WAVES, 128)
    turned = lax.dot_general(fields_ref[...], rows, NT, preferred_element_type=F32).astype(BF16)
    place = lax.broadcasted_iota(jnp.int32, (WAVES, WAVES), 0)
    chosen = (place == slots_ref[...]).astype(F32).astype(BF16)
    ordered = lax.dot_general(turned, chosen, NT, preferred_element_type=F32)
    real, imag = ordered[:FL], ordered[FL:]
    for q in range(4):
        alpha, beta = turns_ref[q : q + 1, :], turns_ref[4 + q : 5 + q, :]
        here = pl.ds(q * FL, FL)
        left_ref[here, :WAVES] = (real * alpha - imag * beta).astype(BF16)
        left_ref[here, WAVES:] = (imag * alpha + real * beta).astype(BF16)
    for w in range(4):
        part = jnp.dot(
            left_ref[...],
            table_ref[:, w * WINDOW : (w + 1) * WINDOW],
            preferred_element_type=F32,
        ).astype(BF16)
        for q in range(4):
            out_ref[4 * q + w] = part[q * FL : (q + 1) * FL]


def band(target, first, count):
    offset = lax.broadcasted_iota(jnp.int32, (count, 128), 0) + (first - 96)
    distance = jnp.abs(offset.astype(F32).astype(BF16) - target.astype(BF16))
    inner = 0.875 - 0.625 * distance
    outer = jnp.minimum(0.0625 * distance - 0.15625, 0.0)
    return jnp.maximum(inner, outer).astype(BF16)


def depart_kernel(target_ref, top_ref, grid_ref, bottom_ref, out_ref, *bands):
    for held in bands:
        held[...] = jnp.zeros_like(held)
    count = out_ref.shape[0]

    def one_row(row, sources):
        for t, (lanes, last) in enumerate(((256, 176), (256, 176), (128, 112))):
            for step in range(3):
                target = target_ref[row, step : step + 1, t * 128 : (t + 1) * 128]
                target = jnp.broadcast_to(target, (last - 16, 128))
                bands[t][step * lanes + 16 : step * lanes + last, :] = band(target, 16, last - 16)
            left = jnp.concatenate([s[:, t * 128 : t * 128 + lanes] for s in sources], axis=1)
            out = jnp.dot(left, bands[t][...], preferred_element_type=F32).astype(BF16)
            width = min(128, BLOCK - t * 128)
            out_ref[row, :, t * 128 : t * 128 + width] = out[:, :width]

    one_row(0, (top_ref, grid_ref.at[0], grid_ref.at[1]))

    @pl.loop(1, count - 1)
    def _(row):
        one_row(row, (grid_ref.at[row - 1], grid_ref.at[row], grid_ref.at[row + 1]))

    one_row(count - 1, (grid_ref.at[count - 2], grid_ref.at[count - 1], bottom_ref))


def send_rows(legendre, spectral):
    rows = legendre.reshape(PAIRS, N_AA, KPACK)
    values = spectral.transpose(0, 2, 3, 1).reshape(PAIRS, 8, KPACK)
    packed = jnp.concatenate(
        [
            rows[:N_BA],
            rows[N_BA:].reshape(N_BA, 8, KPACK),
            values[:N_BA],
            jnp.repeat(values[N_BA:], 4, axis=0),
        ],
        axis=1,
    )
    return jnp.pad(packed, ((0, 0), (0, 0), (0, KPAD - KPACK)))


def legendre_sums(pairs, rows):
    return pl.pallas_call(
        legendre_kernel,
        out_shape=jax.ShapeDtypeStruct((N_BA, 40, 256), BF16),
        in_specs=[pl.BlockSpec(memory_space=pltpu.SMEM)] + whole(1),
        out_specs=whole(1)[0],
        compiler_params=params(24),
        name="legendre_sums",
    )(pairs, rows)


def synthesize(slots, coefficients):
    return pl.pallas_call(
        synthesis_kernel,
        out_shape=jax.ShapeDtypeStruct((N_BA, FL, WINDOW), BF16),
        in_specs=whole(5),
        out_specs=whole(1)[0],
        scratch_shapes=[pltpu.VMEM((4 * FL, 2 * WAVES), BF16)],
        compiler_params=params(32),
        name="synthesize",
    )(
        slots,
        jnp.asarray(quarter_turns()),
        jnp.asarray(field_order()),
        coefficients,
        jnp.asarray(window_table()),
    )


def depart(targets, top, grid, bottom):
    return pl.pallas_call(
        depart_kernel,
        out_shape=jax.ShapeDtypeStruct((N_BA, FL, BLOCK), BF16),
        in_specs=whole(4),
        out_specs=whole(1)[0],
        scratch_shapes=[
            pltpu.VMEM((768, 128), BF16),
            pltpu.VMEM((768, 128), BF16),
            pltpu.VMEM((384, 128), BF16),
        ],
        compiler_params=params(24),
        name="depart",
    )(targets, top, grid, bottom)


def depart_targets(lat_shift, lon_shift):
    x = jnp.arange(BLOCK, dtype=jnp.int32) % 128
    centre = (x + lon_shift).astype(F32) + (HALO - 1 + 1.5 - 96)
    targets = jnp.stack([jnp.where(lat_shift == s, centre, FAR) for s in (-1, 0, 1)], axis=1)
    return jnp.pad(targets, ((0, 0), (0, 0), (0, WINDOW - BLOCK)), constant_values=FAR)


def wave_places(slot_pairs):
    places = slot_pairs.reshape(N_AA, 1, PAIRS) + (jnp.arange(2) * (WAVES // 2))[None, :, None]
    return places.reshape(1, WAVES).astype(jnp.int32)


def local(legendre, spectral, slot_pairs, lat_shift, lon_shift):
    first = lax.axis_index("aa") * PAIRS
    own = lax.axis_index("ba")
    pairs = jnp.stack([slot_pairs[first + own], slot_pairs[first + N_BA + own // 4]])
    rows = lax.all_to_all(send_rows(legendre, spectral), "ba", 0, 0, tiled=True)
    sums = lax.all_to_all(legendre_sums(pairs, rows), "ba", 0, 0, tiled=True)
    by_pair = jnp.concatenate([sums[:, :N_AA], sums[:, N_AA:].reshape(4, N_AA, 256)], axis=0)
    by_row = by_pair.reshape(PAIRS, N_AA, 2, 128).transpose(1, 2, 0, 3).reshape(N_AA, 40, 128)
    coefficients = lax.all_to_all(by_row, "aa", 0, 0, tiled=True)
    blocks = synthesize(wave_places(slot_pairs), coefficients)
    grid = lax.all_to_all(blocks, "ba", 0, 0, tiled=True)
    ends = N_AA - 1
    top = lax.ppermute(grid[N_BA - 1], "aa", [(i, i + 1) for i in range(ends)])
    bottom = lax.ppermute(grid[0], "aa", [(i + 1, i) for i in range(ends)])
    return depart(depart_targets(lat_shift, lon_shift), top, grid, bottom)


def solution(mesh):
    placed = (
        P("aa", None, "ba", None, None),
        P("aa", None, None, "ba"),
        P(),
        P("aa", "ba"),
        P("aa", "ba"),
    )
    return jax.shard_map(
        local, mesh=mesh, in_specs=placed, out_specs=P("aa", None, "ba"), check_vma=False
    )
```

```python
import math

import jax
import jax.numpy as jnp
import numpy as np
from jax import lax
from jax.experimental import pallas as pl
from jax.experimental.pallas import tpu as pltpu
from jax.sharding import PartitionSpec as P

WAVES = 1280
NLON = 5120
FL = 64
KPACK = 1281
KTILES = 10
TILES = 7 * KTILES + 1
N_AA = 32
N_BA = 16
PAIRS = 20
HALO = 32
QUARTER = NLON // 4
BLOCK = NLON // N_BA
WINDOW = BLOCK + 2 * HALO
BF16 = jnp.bfloat16
F32 = jnp.float32
NT = (((1,), (1,)), ((), ()))
FAR = -1000.0


def params(mib):
    return pltpu.CompilerParams(vmem_limit_bytes=mib * 1024 * 1024)


def whole(count):
    return [pl.BlockSpec(memory_space=pltpu.VMEM)] * count


def wave_order():
    pairs = np.arange(WAVES // 2)
    return np.concatenate([pairs, WAVES - 1 - pairs])


def window_table():
    starts = np.arange(2)[:, None] * BLOCK - HALO
    lons = (starts + np.arange(WINDOW)[None, :]).reshape(-1)
    phases = wave_order()[:, None] * lons[None, :] % NLON
    angles = phases.astype(np.float32) * np.float32(2.0 * math.pi / NLON)
    factor = np.float32(1.0 / math.sqrt(WAVES))
    table = np.stack([np.cos(angles) * factor, -np.sin(angles) * factor], axis=0)
    return table.astype(np.float32).astype(BF16)


def mirror():
    x = np.arange(WINDOW)
    return (x[:, None] + x[None, :] == WINDOW).astype(np.float32).astype(BF16)


def quarter_turns():
    turns = wave_order()[None, :] * np.arange(4)[:, None] % 4
    real = np.array([1, 0, -1, 0])[turns]
    imag = np.array([0, 1, 0, -1])[turns]
    return np.concatenate([real, imag], axis=0).astype(np.float32)


def field_order():
    c, b, f4 = np.meshgrid(np.arange(2), np.arange(N_BA), np.arange(4), indexing="ij")
    lanes = (b * 8 + c * 4 + f4).reshape(-1)
    return (lanes[:, None] == np.arange(128)[None, :]).astype(np.float32).astype(BF16)


def pack_kernel(main_ref, shared_ref, main_values_ref, shared_values_ref, out_ref):
    lane = lax.broadcasted_iota(jnp.int32, (8, 128), 1)
    for h in range(4):
        last = jnp.zeros((8, 128), F32)
        for g in range(7):
            for k in range(KTILES + 1):
                here = slice(128 * k, min(128 * k + 128, KPACK))
                if g < 4:
                    tile = main_ref[h, 8 * g : 8 * g + 8, here]
                elif g == 4:
                    tile = shared_ref[0, 8 * h : 8 * h + 8, here]
                else:
                    ref, at = ((main_values_ref, h), (shared_values_ref, 0))[g - 5]
                    tile = ref[at, :, :, here].reshape(8, here.stop - here.start)
                if k < KTILES:
                    out_ref[h, 7 * k + g] = tile
                else:
                    column = jnp.broadcast_to(tile.astype(F32), (8, 128))
                    last = jnp.where(lane == g, column, last)
        out_ref[h, TILES - 1] = last.astype(BF16)


def legendre_kernel(pairs_ref, rows_ref, out_ref):
    column = lax.broadcasted_iota(jnp.int32, (1, 128 * KTILES), 1)
    lane = lax.broadcasted_iota(jnp.int32, (1, 128), 1)
    last = rows_ref[:, TILES - 1]
    for which, (first, count, value) in enumerate(((0, 4, 5), (4, 1, 6))):
        total = N_BA * 8 * count
        left = [
            rows_ref[:, 7 * k + first : 7 * k + first + count].reshape(total, 128)
            for k in range(KTILES)
        ]
        ends = [last * (lane == first + g).astype(F32).astype(BF16) for g in range(count)]
        left.append(jnp.stack(ends, axis=1).reshape(total, 128))
        values = [rows_ref[:, 7 * k + value].reshape(128, 128) for k in range(KTILES)]
        values = jnp.concatenate(values, axis=1)
        end = last.reshape(128, 128)[:, value : value + 1].astype(F32)
        end = jnp.broadcast_to(end, (128, 128)).astype(BF16)
        lower = (column < WAVES - pairs_ref[which]).astype(F32)
        right = jnp.concatenate(
            [
                jnp.concatenate([values * lower.astype(BF16), jnp.zeros_like(end)], axis=1),
                jnp.concatenate([values * (1.0 - lower).astype(BF16), end], axis=1),
            ],
            axis=0,
        )
        left = jnp.concatenate(left, axis=1)
        out = lax.dot_general(left, right, NT, preferred_element_type=F32).astype(BF16)
        out_ref[:, 8 * first : 8 * (first + count), :] = out.reshape(N_BA, 8 * count, 256)


def synthesis_kernel(
    chosen_ref, turns_ref, fields_ref, mirror_ref, coef_ref, table_ref, out_ref, left_ref, held_ref, sems
):
    copies = [
        pltpu.make_async_copy(table_ref.at[c], held_ref.at[c], sems.at[c]) for c in range(2)
    ]
    for copy in copies:
        copy.start()
    rows = coef_ref[...].reshape(WAVES, 128)
    turned = lax.dot_general(fields_ref[...], rows, NT, preferred_element_type=F32).astype(BF16)
    ordered = lax.dot_general(turned, chosen_ref[...], NT, preferred_element_type=F32)
    real, imag = ordered[:FL], ordered[FL:]
    for q in range(4):
        alpha, beta = turns_ref[q : q + 1, :], turns_ref[4 + q : 5 + q, :]
        here = pl.ds(q * FL, FL)
        left_ref[0, here, :] = (real * alpha - imag * beta).astype(BF16)
        left_ref[1, here, :] = (imag * alpha + real * beta).astype(BF16)
    copies[0].wait()
    even = jnp.dot(left_ref[0], held_ref[0], preferred_element_type=F32)
    copies[1].wait()
    odd = jnp.dot(left_ref[1], held_ref[1], preferred_element_type=F32)
    ahead, behind = (even + odd).astype(BF16), (even - odd).astype(BF16)
    for w in range(2):
        lanes = slice(w * WINDOW, (w + 1) * WINDOW)
        back = jnp.dot(behind[:, lanes], mirror_ref[...], preferred_element_type=F32).astype(BF16)
        for q in range(4):
            here = slice(q * FL, (q + 1) * FL)
            out_ref[4 * q + w] = ahead[here, lanes]
            out_ref[(4 * q + N_BA - 1 - w) % N_BA] = back[here]


def band(target, first, count):
    offset = lax.broadcasted_iota(jnp.int32, (count, 128), 0) + (first - 96)
    distance = jnp.abs(offset.astype(F32).astype(BF16) - target.astype(BF16))
    inner = 0.875 - 0.625 * distance
    outer = jnp.minimum(0.0625 * distance - 0.15625, 0.0)
    return jnp.maximum(inner, outer).astype(BF16)


def clear(bands):
    for held in bands:
        held[...] = jnp.zeros_like(held)


def depart_row(target_ref, at, sources, bands, out_ref, to):
    for t, (part, lanes, last, first) in enumerate(((0, 384, 176, 0), (0, 384, 176, 128), (1, 128, 112, 0))):
        for step in range(3):
            target = target_ref[at, step : step + 1, t * 128 : (t + 1) * 128]
            target = jnp.broadcast_to(target, (last - 16, 128))
            begin = step * lanes + first + 16
            bands[part][begin : begin + last - 16, first : first + 128] = band(target, 16, last - 16)
    for part, (lane, x, width) in enumerate(((0, 0, 256), (256, 256, 64))):
        left = jnp.concatenate([s[:, lane:] for s in sources], axis=1)
        out = jnp.dot(left, bands[part][...], preferred_element_type=F32).astype(BF16)
        out_ref[to, :, x : x + width] = out[:, :width]


def inner_kernel(target_ref, grid_ref, out_ref, *bands):
    clear(bands)

    @pl.loop(1, N_BA - 1, unroll=7)
    def _(row):
        sources = [grid_ref.at[row - 1], grid_ref.at[row], grid_ref.at[row + 1]]
        depart_row(target_ref, row, sources, bands, out_ref, row)


def edge_kernel(inner_ref, target_ref, top_ref, grid_ref, bottom_ref, out_ref, *bands):
    clear(bands)

    @pl.when(pl.program_id(0) == 0)
    def _():
        sources = [top_ref, grid_ref.at[0], grid_ref.at[1]]
        depart_row(target_ref, 0, sources, bands, out_ref, 0)

    @pl.when(pl.program_id(0) == 1)
    def _():
        sources = [grid_ref.at[N_BA - 2], grid_ref.at[N_BA - 1], bottom_ref]
        depart_row(target_ref, N_BA - 1, sources, bands, out_ref, 0)


def pack(legendre, spectral):
    rows = legendre.reshape(PAIRS, N_AA, KPACK)
    values = spectral.transpose(0, 2, 3, 1)
    return pl.pallas_call(
        pack_kernel,
        grid=(4,),
        out_shape=jax.ShapeDtypeStruct((N_BA, TILES, 8, 128), BF16),
        in_specs=[
            pl.BlockSpec((4, N_AA, KPACK), lambda q: (q, 0, 0)),
            pl.BlockSpec((1, N_AA, KPACK), lambda q: (N_BA + q, 0, 0)),
            pl.BlockSpec((4, 2, 4, KPACK), lambda q: (q, 0, 0, 0)),
            pl.BlockSpec((1, 2, 4, KPACK), lambda q: (N_BA + q, 0, 0, 0)),
        ],
        out_specs=pl.BlockSpec((4, TILES, 8, 128), lambda q: (q, 0, 0, 0)),
        compiler_params=params(58),
        name="pack",
    )(rows, rows, values, values)


def legendre_sums(pairs, rows):
    return pl.pallas_call(
        legendre_kernel,
        out_shape=jax.ShapeDtypeStruct((N_BA, 40, 256), BF16),
        in_specs=[pl.BlockSpec(memory_space=pltpu.SMEM)] + whole(1),
        out_specs=whole(1)[0],
        compiler_params=params(24),
        name="legendre_sums",
    )(pairs, rows)


def synthesize(chosen, coefficients):
    return pl.pallas_call(
        synthesis_kernel,
        out_shape=jax.ShapeDtypeStruct((N_BA, FL, WINDOW), BF16),
        in_specs=whole(5) + [pl.BlockSpec(memory_space=pl.ANY)],
        out_specs=whole(1)[0],
        scratch_shapes=[
            pltpu.VMEM((2, 4 * FL, WAVES), BF16),
            pltpu.VMEM((2, WAVES, 2 * WINDOW), BF16),
            pltpu.SemaphoreType.DMA((2,)),
        ],
        compiler_params=params(32),
        name="synthesize",
    )(
        chosen,
        jnp.asarray(quarter_turns()),
        jnp.asarray(field_order()),
        jnp.asarray(mirror()),
        coefficients,
        jnp.asarray(window_table()),
    )


def band_scratch():
    return [pltpu.VMEM((1152, 256), BF16), pltpu.VMEM((384, 128), BF16)]


def depart_inner(targets, grid):
    return pl.pallas_call(
        inner_kernel,
        out_shape=jax.ShapeDtypeStruct((N_BA, FL, BLOCK), BF16),
        in_specs=whole(2),
        out_specs=whole(1)[0],
        scratch_shapes=band_scratch(),
        compiler_params=params(24),
        cost_estimate=pl.CostEstimate(
            flops=2 * 14 * FL * 1920 * 128, bytes_accessed=4000000, transcendentals=0
        ),
        name="depart_inner",
    )(targets, grid)


def depart_edges(inner, targets, top, grid, bottom):
    return pl.pallas_call(
        edge_kernel,
        grid=(2,),
        out_shape=jax.ShapeDtypeStruct((N_BA, FL, BLOCK), BF16),
        in_specs=[pl.BlockSpec(memory_space=pl.ANY)] + whole(4),
        out_specs=pl.BlockSpec((1, FL, BLOCK), lambda e: (e * (N_BA - 1), 0, 0)),
        scratch_shapes=band_scratch(),
        input_output_aliases={0: 0},
        compiler_params=params(24),
        name="depart_edges",
    )(inner, targets, top, grid, bottom)


def depart_targets(lat_shift, lon_shift):
    x = jnp.arange(BLOCK, dtype=jnp.int32) % 128
    centre = (x + lon_shift).astype(F32) + (HALO - 1 + 1.5 - 96)
    targets = jnp.stack([jnp.where(lat_shift == s, centre, FAR) for s in (-1, 0, 1)], axis=1)
    return jnp.pad(targets, ((0, 0), (0, 0), (0, WINDOW - BLOCK)), constant_values=FAR)


def wave_places(slot_pairs):
    places = slot_pairs.reshape(N_AA, 1, PAIRS) + (jnp.arange(2) * (WAVES // 2))[None, :, None]
    places = places.reshape(1, WAVES).astype(jnp.int32)
    return (jnp.arange(WAVES, dtype=jnp.int32)[:, None] == places).astype(BF16)


def local(legendre, spectral, slot_pairs, lat_shift, lon_shift):
    first = lax.axis_index("aa") * PAIRS
    own = lax.axis_index("ba")
    pairs = jnp.stack([slot_pairs[first + own], slot_pairs[first + N_BA + own // 4]])
    rows = lax.all_to_all(pack(legendre, spectral), "ba", 0, 0, tiled=True)
    sums = lax.all_to_all(legendre_sums(pairs, rows), "ba", 0, 0, tiled=True)
    by_pair = jnp.concatenate([sums[:, :N_AA], sums[:, N_AA:].reshape(4, N_AA, 256)], axis=0)
    by_row = by_pair.reshape(PAIRS, N_AA, 2, 128).transpose(1, 2, 0, 3).reshape(N_AA, 40, 128)
    coefficients = lax.all_to_all(by_row, "aa", 0, 0, tiled=True)
    blocks = synthesize(wave_places(slot_pairs), coefficients)
    grid = lax.all_to_all(blocks, "ba", 0, 0, tiled=True)
    ends = N_AA - 1
    top = lax.ppermute(grid[N_BA - 1], "aa", [(i, i + 1) for i in range(ends)])
    bottom = lax.ppermute(grid[0], "aa", [(i + 1, i) for i in range(ends)])
    targets = depart_targets(lat_shift, lon_shift)
    inner = depart_inner(targets, grid)
    return depart_edges(inner, targets, top, grid, bottom)


def solution(mesh):
    placed = (
        P("aa", None, "ba", None, None),
        P("aa", None, None, "ba"),
        P(),
        P("aa", "ba"),
        P("aa", "ba"),
    )
    return jax.shard_map(
        local, mesh=mesh, in_specs=placed, out_specs=P("aa", None, "ba"), check_vma=False
    )
```

```python
import math

import jax
import jax.numpy as jnp
import numpy as np
from jax import lax
from jax.experimental import pallas as pl
from jax.experimental.pallas import tpu as pltpu
from jax.sharding import PartitionSpec as P

WAVES = 1280
NLON = 5120
FL = 64
KPACK = 1281
KTILES = 10
TILES = 7 * KTILES + 1
N_AA = 32
N_BA = 16
PAIRS = 20
HALO = 32
QUARTER = NLON // 4
BLOCK = NLON // N_BA
WINDOW = BLOCK + 2 * HALO
BF16 = jnp.bfloat16
F32 = jnp.float32
NT = (((1,), (1,)), ((), ()))
FAR = -1000.0


def params(mib):
    return pltpu.CompilerParams(vmem_limit_bytes=mib * 1024 * 1024)


def whole(count):
    return [pl.BlockSpec(memory_space=pltpu.VMEM)] * count


def wave_order():
    pairs = np.arange(WAVES // 2)
    return np.concatenate([pairs, WAVES - 1 - pairs])


def window_table():
    starts = np.arange(2)[:, None] * BLOCK - HALO
    lons = (starts + np.arange(WINDOW)[None, :]).reshape(-1)
    phases = wave_order()[:, None] * lons[None, :] % NLON
    angles = phases.astype(np.float32) * np.float32(2.0 * math.pi / NLON)
    factor = np.float32(1.0 / math.sqrt(WAVES))
    table = np.stack([np.cos(angles) * factor, -np.sin(angles) * factor], axis=0)
    return table.astype(np.float32).astype(BF16)


def pack_kernel(rows_ref, values_ref, out_ref, rows_held, values_held, out_held, sems):
    into = [pltpu.make_async_copy(values_ref, values_held, sems.at[PAIRS])]
    for pair in [i for q in range(4) for i in (N_BA + q, 4 * q, 4 * q + 1, 4 * q + 2, 4 * q + 3)]:
        into.append(pltpu.make_async_copy(rows_ref.at[pair], rows_held.at[pair], sems.at[pair]))
    for copy in into:
        copy.start()
    into[0].wait()
    out = []
    lane = lax.broadcasted_iota(jnp.int32, (8, 128), 1)
    for d in range(N_BA):
        q, h = d // 4, d % 4
        if h == 0:
            into[1 + 5 * q].wait()
        into[2 + 5 * q + h].wait()
        last = jnp.zeros((8, 128), F32)
        for g in range(7):
            for k in range(KTILES + 1):
                here = slice(128 * k, min(128 * k + 128, KPACK))
                if g < 4:
                    tile = rows_held[d, 8 * g : 8 * g + 8, here]
                elif g == 4:
                    tile = rows_held[N_BA + q, 8 * h : 8 * h + 8, here]
                else:
                    pair = (d, N_BA + q)[g - 5]
                    tile = values_held[pair, :, :, here].reshape(8, here.stop - here.start)
                if k < KTILES:
                    out_held[d, 7 * k + g] = tile
                else:
                    column = jnp.broadcast_to(tile.astype(F32), (8, 128))
                    last = jnp.where(lane == g, column, last)
        out_held[d, TILES - 1] = last.astype(BF16)
        out.append(pltpu.make_async_copy(out_held.at[d], out_ref.at[d], sems.at[PAIRS + 1 + d]))
        out[-1].start()
    for copy in out:
        copy.wait()


def legendre_kernel(pairs_ref, rows_ref, out_ref):
    column = lax.broadcasted_iota(jnp.int32, (1, 128 * KTILES), 1)
    lane = lax.broadcasted_iota(jnp.int32, (1, 128), 1)
    last = rows_ref[:, TILES - 1]
    for which, (first, count, value) in enumerate(((0, 4, 5), (4, 1, 6))):
        total = N_BA * 8 * count
        left = [
            rows_ref[:, 7 * k + first : 7 * k + first + count].reshape(total, 128)
            for k in range(KTILES)
        ]
        ends = [last * (lane == first + g).astype(F32).astype(BF16) for g in range(count)]
        left.append(jnp.stack(ends, axis=1).reshape(total, 128))
        values = [rows_ref[:, 7 * k + value].reshape(128, 128) for k in range(KTILES)]
        values = jnp.concatenate(values, axis=1)
        end = last.reshape(128, 128)[:, value : value + 1].astype(F32)
        end = jnp.broadcast_to(end, (128, 128)).astype(BF16)
        lower = (column < WAVES - pairs_ref[which]).astype(F32)
        right = jnp.concatenate(
            [
                jnp.concatenate([values * lower.astype(BF16), jnp.zeros_like(end)], axis=1),
                jnp.concatenate([values * (1.0 - lower).astype(BF16), end], axis=1),
            ],
            axis=0,
        )
        left = jnp.concatenate(left, axis=1)
        out = lax.dot_general(left, right, NT, preferred_element_type=F32).astype(BF16)
        out_ref[:, 8 * first : 8 * (first + count), :] = out.reshape(N_BA, 8 * count, 256)


def iota(shape, dim):
    return lax.broadcasted_iota(jnp.int32, shape, dim)


def ones_where(chosen):
    return chosen.astype(F32).astype(BF16)


def synthesis_kernel(
    places_ref, coef_ref, table_ref, out_ref, rows_ref, left_ref, held_ref, blocks_ref, sems
):
    arriving = pltpu.make_async_copy(coef_ref, rows_ref, sems.at[2 + N_BA])
    arriving.start()
    copies = [
        pltpu.make_async_copy(table_ref.at[c], held_ref.at[c], sems.at[c]) for c in range(2)
    ]
    for copy in copies:
        copy.start()
    row, lane = iota((128, 128), 0), iota((128, 128), 1)
    fields = ones_where(lane == (row % FL) // 4 * 8 + row // FL * 4 + row % 4)
    chosen = ones_where(iota((WAVES, WAVES), 0) == places_ref[...])
    arriving.wait()
    rows = rows_ref[...].reshape(WAVES, 128)
    turned = lax.dot_general(fields, rows, NT, preferred_element_type=F32).astype(BF16)
    ordered = lax.dot_general(turned, chosen, NT, preferred_element_type=F32)
    real, imag = ordered[:FL], ordered[FL:]
    place = iota((1, WAVES), 1)
    wave = jnp.where(place < WAVES // 2, place, WAVES + WAVES // 2 - 1 - place)
    for q in range(4):
        turn = wave * q % 4
        alpha = (turn == 0).astype(F32) - (turn == 2).astype(F32)
        beta = (turn == 1).astype(F32) - (turn == 3).astype(F32)
        here = pl.ds(q * FL, FL)
        left_ref[0, here, :] = (real * alpha - imag * beta).astype(BF16)
        left_ref[1, here, :] = (imag * alpha + real * beta).astype(BF16)
    copies[0].wait()
    even = jnp.dot(left_ref[0], held_ref[0], preferred_element_type=F32)
    copies[1].wait()
    odd = jnp.dot(left_ref[1], held_ref[1], preferred_element_type=F32)
    ahead, behind = (even + odd).astype(BF16), (even - odd).astype(BF16)
    mirror = ones_where(iota((WINDOW, WINDOW), 0) + iota((WINDOW, WINDOW), 1) == WINDOW)
    sent = []

    def finish(block, value):
        blocks_ref[block] = value
        sent.append(pltpu.make_async_copy(blocks_ref.at[block], out_ref.at[block], sems.at[2 + block]))
        sent[-1].start()

    for w in range(2):
        lanes = slice(w * WINDOW, (w + 1) * WINDOW)
        back = jnp.dot(behind[:, lanes], mirror, preferred_element_type=F32).astype(BF16)
        for q in range(4):
            here = slice(q * FL, (q + 1) * FL)
            finish(4 * q + w, ahead[here, lanes])
            finish((4 * q + N_BA - 1 - w) % N_BA, back[here])
    for copy in sent:
        copy.wait()


def band(target, first, count):
    offset = lax.broadcasted_iota(jnp.int32, (count, 128), 0) + (first - 96)
    distance = jnp.abs(offset.astype(F32).astype(BF16) - target.astype(BF16))
    inner = 0.875 - 0.625 * distance
    outer = jnp.minimum(0.0625 * distance - 0.15625, 0.0)
    return jnp.maximum(inner, outer).astype(BF16)


def clear(bands):
    for held in bands:
        held[...] = jnp.zeros_like(held)


def depart_row(target_ref, at, sources, bands, out_ref, to):
    for t, (part, lanes, last, first) in enumerate(((0, 384, 176, 0), (0, 384, 176, 128), (1, 128, 112, 0))):
        for step in range(3):
            target = target_ref[at, step : step + 1, t * 128 : (t + 1) * 128]
            target = jnp.broadcast_to(target, (last - 16, 128))
            begin = step * lanes + first + 16
            bands[part][begin : begin + last - 16, first : first + 128] = band(target, 16, last - 16)
    for part, (lane, x, width) in enumerate(((0, 0, 256), (256, 256, 64))):
        left = jnp.concatenate([s[:, lane:] for s in sources], axis=1)
        out = jnp.dot(left, bands[part][...], preferred_element_type=F32).astype(BF16)
        out_ref[to, :, x : x + width] = out[:, :width]


def inner_kernel(target_ref, grid_ref, out_ref, *bands):
    clear(bands)

    @pl.loop(1, N_BA - 1, unroll=7)
    def _(row):
        sources = [grid_ref.at[row - 1], grid_ref.at[row], grid_ref.at[row + 1]]
        depart_row(target_ref, row, sources, bands, out_ref, row)


def edge_kernel(inner_ref, target_ref, top_ref, grid_ref, bottom_ref, out_ref, *bands):
    clear(bands)

    @pl.when(pl.program_id(0) == 0)
    def _():
        sources = [top_ref, grid_ref.at[0], grid_ref.at[1]]
        depart_row(target_ref, 0, sources, bands, out_ref, 0)

    @pl.when(pl.program_id(0) == 1)
    def _():
        sources = [grid_ref.at[N_BA - 2], grid_ref.at[N_BA - 1], bottom_ref]
        depart_row(target_ref, N_BA - 1, sources, bands, out_ref, 0)


def pack(legendre, spectral):
    rows = legendre.reshape(PAIRS, N_AA, KPACK)
    values = spectral.transpose(0, 2, 3, 1)
    anywhere = pl.BlockSpec(memory_space=pl.ANY)
    return pl.pallas_call(
        pack_kernel,
        out_shape=jax.ShapeDtypeStruct((N_BA, TILES, 8, 128), BF16),
        in_specs=[anywhere, anywhere],
        out_specs=anywhere,
        scratch_shapes=[
            pltpu.VMEM((PAIRS, N_AA, KPACK), BF16),
            pltpu.VMEM((PAIRS, 2, 4, KPACK), BF16),
            pltpu.VMEM((N_BA, TILES, 8, 128), BF16),
            pltpu.SemaphoreType.DMA((PAIRS + 1 + N_BA,)),
        ],
        compiler_params=params(59),
        name="pack",
    )(rows, values)


def legendre_sums(pairs, rows):
    return pl.pallas_call(
        legendre_kernel,
        out_shape=jax.ShapeDtypeStruct((N_BA, 40, 256), BF16),
        in_specs=[pl.BlockSpec(memory_space=pltpu.SMEM)] + whole(1),
        out_specs=whole(1)[0],
        compiler_params=params(24),
        name="legendre_sums",
    )(pairs, rows)


def synthesize(places, coefficients):
    anywhere = pl.BlockSpec(memory_space=pl.ANY)
    return pl.pallas_call(
        synthesis_kernel,
        out_shape=jax.ShapeDtypeStruct((N_BA, FL, WINDOW), BF16),
        in_specs=whole(1) + [anywhere] * 2,
        out_specs=anywhere,
        scratch_shapes=[
            pltpu.VMEM((N_AA, 40, 128), BF16),
            pltpu.VMEM((2, 4 * FL, WAVES), BF16),
            pltpu.VMEM((2, WAVES, 2 * WINDOW), BF16),
            pltpu.VMEM((N_BA, FL, WINDOW), BF16),
            pltpu.SemaphoreType.DMA((3 + N_BA,)),
        ],
        compiler_params=params(59),
        name="synthesize",
    )(places, coefficients, jnp.asarray(window_table()))


def band_scratch():
    return [pltpu.VMEM((1152, 256), BF16), pltpu.VMEM((384, 128), BF16)]


def depart_inner(targets, grid):
    return pl.pallas_call(
        inner_kernel,
        out_shape=jax.ShapeDtypeStruct((N_BA, FL, BLOCK), BF16),
        in_specs=whole(2),
        out_specs=whole(1)[0],
        scratch_shapes=band_scratch(),
        compiler_params=params(24),
        cost_estimate=pl.CostEstimate(
            flops=2 * 14 * FL * 1920 * 128, bytes_accessed=4000000, transcendentals=0
        ),
        name="depart_inner",
    )(targets, grid)


def depart_edges(inner, targets, top, grid, bottom):
    return pl.pallas_call(
        edge_kernel,
        grid=(2,),
        out_shape=jax.ShapeDtypeStruct((N_BA, FL, BLOCK), BF16),
        in_specs=[pl.BlockSpec(memory_space=pl.ANY)] + whole(4),
        out_specs=pl.BlockSpec((1, FL, BLOCK), lambda e: (e * (N_BA - 1), 0, 0)),
        scratch_shapes=band_scratch(),
        input_output_aliases={0: 0},
        compiler_params=params(24),
        name="depart_edges",
    )(inner, targets, top, grid, bottom)


def depart_targets(lat_shift, lon_shift):
    x = jnp.arange(BLOCK, dtype=jnp.int32) % 128
    centre = (x + lon_shift).astype(F32) + (HALO - 1 + 1.5 - 96)
    targets = jnp.stack([jnp.where(lat_shift == s, centre, FAR) for s in (-1, 0, 1)], axis=1)
    return jnp.pad(targets, ((0, 0), (0, 0), (0, WINDOW - BLOCK)), constant_values=FAR)


def wave_places(slot_pairs):
    places = slot_pairs.reshape(N_AA, 1, PAIRS) + (jnp.arange(2) * (WAVES // 2))[None, :, None]
    return places.reshape(1, WAVES).astype(jnp.int32)


def local(legendre, spectral, slot_pairs, lat_shift, lon_shift):
    first = lax.axis_index("aa") * PAIRS
    own = lax.axis_index("ba")
    pairs = jnp.stack([slot_pairs[first + own], slot_pairs[first + N_BA + own // 4]])
    rows = lax.all_to_all(pack(legendre, spectral), "ba", 0, 0, tiled=True)
    sums = lax.all_to_all(legendre_sums(pairs, rows), "ba", 0, 0, tiled=True)
    by_pair = jnp.concatenate([sums[:, :N_AA], sums[:, N_AA:].reshape(4, N_AA, 256)], axis=0)
    by_row = by_pair.reshape(PAIRS, N_AA, 2, 128).transpose(1, 2, 0, 3).reshape(N_AA, 40, 128)
    coefficients = lax.all_to_all(by_row, "aa", 0, 0, tiled=True)
    blocks = synthesize(wave_places(slot_pairs), coefficients)
    grid = lax.all_to_all(blocks, "ba", 0, 0, tiled=True)
    ends = N_AA - 1
    top = lax.ppermute(grid[N_BA - 1], "aa", [(i, i + 1) for i in range(ends)])
    bottom = lax.ppermute(grid[0], "aa", [(i + 1, i) for i in range(ends)])
    targets = depart_targets(lat_shift, lon_shift)
    inner = depart_inner(targets, grid)
    return depart_edges(inner, targets, top, grid, bottom)


def solution(mesh):
    placed = (
        P("aa", None, "ba", None, None),
        P("aa", None, None, "ba"),
        P(),
        P("aa", "ba"),
        P("aa", "ba"),
    )
    return jax.shard_map(
        local, mesh=mesh, in_specs=placed, out_specs=P("aa", None, "ba"), check_vma=False
    )
```

```python
import math

import jax
import jax.numpy as jnp
import numpy as np
from jax import lax
from jax.experimental import pallas as pl
from jax.experimental.pallas import tpu as pltpu
from jax.sharding import PartitionSpec as P

WAVES = 1280
NLON = 5120
FL = 64
KPACK = 1281
KTILES = 10
TILES = 7 * KTILES + 1
N_AA = 32
N_BA = 16
PAIRS = 20
HALO = 32
QUARTER = NLON // 4
BLOCK = NLON // N_BA
WINDOW = BLOCK + 2 * HALO
BF16 = jnp.bfloat16
F32 = jnp.float32
NT = (((1,), (1,)), ((), ()))
FAR = -1000.0


def params(mib):
    return pltpu.CompilerParams(vmem_limit_bytes=mib * 1024 * 1024)


def whole(count):
    return [pl.BlockSpec(memory_space=pltpu.VMEM)] * count


def wave_order():
    pairs = np.arange(WAVES // 2)
    return np.concatenate([pairs, WAVES - 1 - pairs])


def window_table():
    starts = np.arange(2)[:, None] * BLOCK - HALO
    lons = (starts + np.arange(WINDOW)[None, :]).reshape(-1)
    phases = wave_order()[:, None] * lons[None, :] % NLON
    angles = phases.astype(np.float32) * np.float32(2.0 * math.pi / NLON)
    factor = np.float32(1.0 / math.sqrt(WAVES))
    table = np.stack([np.cos(angles) * factor, -np.sin(angles) * factor], axis=0)
    return table.astype(np.float32).astype(BF16)


def pack_kernel(rows_ref, values_ref, out_ref, rows_held, values_held, out_held, sems):
    into = [pltpu.make_async_copy(values_ref, values_held, sems.at[PAIRS])]
    for pair in [i for q in range(4) for i in (N_BA + q, 4 * q, 4 * q + 1, 4 * q + 2, 4 * q + 3)]:
        into.append(pltpu.make_async_copy(rows_ref.at[pair], rows_held.at[pair], sems.at[pair]))
    for copy in into:
        copy.start()
    into[0].wait()
    out = []
    lane = lax.broadcasted_iota(jnp.int32, (8, 128), 1)
    for d in range(N_BA):
        q, h = d // 4, d % 4
        if h == 0:
            into[1 + 5 * q].wait()
        into[2 + 5 * q + h].wait()
        last = jnp.zeros((8, 128), F32)
        for g in range(7):
            for k in range(KTILES + 1):
                here = slice(128 * k, min(128 * k + 128, KPACK))
                if g < 4:
                    tile = rows_held[d, 8 * g : 8 * g + 8, here]
                elif g == 4:
                    tile = rows_held[N_BA + q, 8 * h : 8 * h + 8, here]
                else:
                    pair = (d, N_BA + q)[g - 5]
                    tile = values_held[pair, :, :, here].reshape(8, here.stop - here.start)
                if k < KTILES:
                    out_held[d, 7 * k + g] = tile
                else:
                    column = jnp.broadcast_to(tile.astype(F32), (8, 128))
                    last = jnp.where(lane == g, column, last)
        out_held[d, TILES - 1] = last.astype(BF16)
        out.append(pltpu.make_async_copy(out_held.at[d], out_ref.at[d], sems.at[PAIRS + 1 + d]))
        out[-1].start()
    for copy in out:
        copy.wait()


def legendre_kernel(pairs_ref, rows_ref, out_ref):
    column = lax.broadcasted_iota(jnp.int32, (1, 128 * KTILES), 1)
    lane = lax.broadcasted_iota(jnp.int32, (1, 128), 1)
    last = rows_ref[:, TILES - 1]
    for which, (first, count, value) in enumerate(((0, 4, 5), (4, 1, 6))):
        total = N_BA * 8 * count
        left = [
            rows_ref[:, 7 * k + first : 7 * k + first + count].reshape(total, 128)
            for k in range(KTILES)
        ]
        ends = [last * (lane == first + g).astype(F32).astype(BF16) for g in range(count)]
        left.append(jnp.stack(ends, axis=1).reshape(total, 128))
        values = [rows_ref[:, 7 * k + value].reshape(128, 128) for k in range(KTILES)]
        values = jnp.concatenate(values, axis=1)
        end = last.reshape(128, 128)[:, value : value + 1].astype(F32)
        end = jnp.broadcast_to(end, (128, 128)).astype(BF16)
        lower = (column < WAVES - pairs_ref[which]).astype(F32)
        right = jnp.concatenate(
            [
                jnp.concatenate([values * lower.astype(BF16), jnp.zeros_like(end)], axis=1),
                jnp.concatenate([values * (1.0 - lower).astype(BF16), end], axis=1),
            ],
            axis=0,
        )
        left = jnp.concatenate(left, axis=1)
        out = lax.dot_general(left, right, NT, preferred_element_type=F32).astype(BF16)
        out_ref[:, 8 * first : 8 * (first + count), :] = out.reshape(N_BA, 8 * count, 256)


def regroup_kernel(perm_ref, sums_ref, out_ref):
    sums = sums_ref[...].reshape(N_BA * 40, 256)
    both = jnp.dot(perm_ref[...], sums, preferred_element_type=F32)
    first = iota((WAVES, 128), 0) // PAIRS % 2 == 0
    out = jnp.where(first, both[:, :128], both[:, 128:]).astype(BF16)
    out_ref[...] = out.reshape(N_AA, 40, 128)


def iota(shape, dim):
    return lax.broadcasted_iota(jnp.int32, shape, dim)


def ones_where(chosen):
    return chosen.astype(F32).astype(BF16)


def synthesis_kernel(
    places_ref, coef_ref, table_ref, out_ref, rows_ref, left_ref, held_ref, blocks_ref, sems
):
    arriving = pltpu.make_async_copy(coef_ref, rows_ref, sems.at[2 + N_BA])
    arriving.start()
    copies = [
        pltpu.make_async_copy(table_ref.at[c], held_ref.at[c], sems.at[c]) for c in range(2)
    ]
    for copy in copies:
        copy.start()
    row, lane = iota((128, 128), 0), iota((128, 128), 1)
    fields = ones_where(lane == (row % FL) // 4 * 8 + row // FL * 4 + row % 4)
    chosen = ones_where(iota((WAVES, WAVES), 0) == places_ref[...])
    arriving.wait()
    rows = rows_ref[...].reshape(WAVES, 128)
    turned = lax.dot_general(fields, rows, NT, preferred_element_type=F32).astype(BF16)
    ordered = lax.dot_general(turned, chosen, NT, preferred_element_type=F32)
    real, imag = ordered[:FL], ordered[FL:]
    place = iota((1, WAVES), 1)
    wave = jnp.where(place < WAVES // 2, place, WAVES + WAVES // 2 - 1 - place)
    for q in range(4):
        turn = wave * q % 4
        alpha = (turn == 0).astype(F32) - (turn == 2).astype(F32)
        beta = (turn == 1).astype(F32) - (turn == 3).astype(F32)
        here = pl.ds(q * FL, FL)
        left_ref[0, here, :] = (real * alpha - imag * beta).astype(BF16)
        left_ref[1, here, :] = (imag * alpha + real * beta).astype(BF16)
    copies[0].wait()
    even = jnp.dot(left_ref[0], held_ref[0], preferred_element_type=F32)
    copies[1].wait()
    odd = jnp.dot(left_ref[1], held_ref[1], preferred_element_type=F32)
    ahead, behind = (even + odd).astype(BF16), (even - odd).astype(BF16)
    mirror = ones_where(iota((WINDOW, WINDOW), 0) + iota((WINDOW, WINDOW), 1) == WINDOW)
    sent = []

    def finish(block, value):
        blocks_ref[block] = value
        sent.append(pltpu.make_async_copy(blocks_ref.at[block], out_ref.at[block], sems.at[2 + block]))
        sent[-1].start()

    for w in range(2):
        lanes = slice(w * WINDOW, (w + 1) * WINDOW)
        back = jnp.dot(behind[:, lanes], mirror, preferred_element_type=F32).astype(BF16)
        for q in range(4):
            here = slice(q * FL, (q + 1) * FL)
            finish(4 * q + w, ahead[here, lanes])
            finish((4 * q + N_BA - 1 - w) % N_BA, back[here])
    for copy in sent:
        copy.wait()


def band(target, first, count):
    offset = lax.broadcasted_iota(jnp.int32, (count, 128), 0) + (first - 96)
    distance = jnp.abs(offset.astype(F32).astype(BF16) - target.astype(BF16))
    inner = 0.875 - 0.625 * distance
    outer = jnp.minimum(0.0625 * distance - 0.15625, 0.0)
    return jnp.maximum(inner, outer).astype(BF16)


def clear(bands):
    for held in bands:
        held[...] = jnp.zeros_like(held)


def depart_row(target_ref, at, sources, bands, out_ref, to):
    for t, (part, lanes, last, first) in enumerate(((0, 384, 176, 0), (0, 384, 176, 128), (1, 128, 112, 0))):
        for step in range(3):
            target = target_ref[at, step : step + 1, t * 128 : (t + 1) * 128]
            target = jnp.broadcast_to(target, (last - 16, 128))
            begin = step * lanes + first + 16
            bands[part][begin : begin + last - 16, first : first + 128] = band(target, 16, last - 16)
    for part, (lane, x, width) in enumerate(((0, 0, 256), (256, 256, 64))):
        left = jnp.concatenate([s[:, lane:] for s in sources], axis=1)
        out = jnp.dot(left, bands[part][...], preferred_element_type=F32).astype(BF16)
        out_ref[to, :, x : x + width] = out[:, :width]


def inner_kernel(target_ref, grid_ref, out_ref, *bands):
    clear(bands)

    @pl.loop(2, N_BA, unroll=7)
    def _(row):
        above = jnp.where(row == N_BA - 1, 0, row + 1)
        sources = [grid_ref.at[row - 1], grid_ref.at[row], grid_ref.at[above]]
        depart_row(target_ref, row, sources, bands, out_ref, row)


def edge_kernel(inner_ref, target_ref, beside_ref, grid_ref, out_ref, *bands):
    clear(bands)
    sources = [beside_ref.at[0], beside_ref.at[1], grid_ref.at[1], grid_ref.at[2]]
    for row in range(2):
        depart_row(target_ref, row, sources[row : row + 3], bands, out_ref, row)


def pack(legendre, spectral):
    rows = legendre.reshape(PAIRS, N_AA, KPACK)
    values = spectral.transpose(0, 2, 3, 1)
    anywhere = pl.BlockSpec(memory_space=pl.ANY)
    return pl.pallas_call(
        pack_kernel,
        out_shape=jax.ShapeDtypeStruct((N_BA, TILES, 8, 128), BF16),
        in_specs=[anywhere, anywhere],
        out_specs=anywhere,
        scratch_shapes=[
            pltpu.VMEM((PAIRS, N_AA, KPACK), BF16),
            pltpu.VMEM((PAIRS, 2, 4, KPACK), BF16),
            pltpu.VMEM((N_BA, TILES, 8, 128), BF16),
            pltpu.SemaphoreType.DMA((PAIRS + 1 + N_BA,)),
        ],
        compiler_params=params(59),
        name="pack",
    )(rows, values)


def legendre_sums(pairs, rows):
    return pl.pallas_call(
        legendre_kernel,
        out_shape=jax.ShapeDtypeStruct((N_BA, 40, 256), BF16),
        in_specs=[pl.BlockSpec(memory_space=pltpu.SMEM)] + whole(1),
        out_specs=whole(1)[0],
        compiler_params=params(24),
        name="legendre_sums",
    )(pairs, rows)


def regroup(perm, sums):
    return pl.pallas_call(
        regroup_kernel,
        out_shape=jax.ShapeDtypeStruct((N_AA, 40, 128), BF16),
        in_specs=whole(2),
        out_specs=whole(1)[0],
        compiler_params=params(24),
        name="regroup",
    )(perm, sums)


def regroup_rows(own):
    row = jnp.arange(WAVES, dtype=jnp.int32)
    lat = (row // 40 + (own == 0).astype(jnp.int32)) % N_AA
    pair = row % PAIRS
    shared = (4 * (pair - N_BA) + lat // 8) * 40 + 32 + lat % 8
    source = jnp.where(pair < N_BA, pair * 40 + lat, shared)
    return (source[:, None] == jnp.arange(N_BA * 40, dtype=jnp.int32)[None, :]).astype(BF16)


def synthesize(places, coefficients):
    anywhere = pl.BlockSpec(memory_space=pl.ANY)
    return pl.pallas_call(
        synthesis_kernel,
        out_shape=jax.ShapeDtypeStruct((N_BA, FL, WINDOW), BF16),
        in_specs=whole(1) + [anywhere] * 2,
        out_specs=anywhere,
        scratch_shapes=[
            pltpu.VMEM((N_AA, 40, 128), BF16),
            pltpu.VMEM((2, 4 * FL, WAVES), BF16),
            pltpu.VMEM((2, WAVES, 2 * WINDOW), BF16),
            pltpu.VMEM((N_BA, FL, WINDOW), BF16),
            pltpu.SemaphoreType.DMA((3 + N_BA,)),
        ],
        compiler_params=params(59),
        name="synthesize",
    )(places, coefficients, jnp.asarray(window_table()))


def band_scratch():
    return [pltpu.VMEM((1152, 256), BF16), pltpu.VMEM((384, 128), BF16)]


def depart_inner(targets, grid):
    return pl.pallas_call(
        inner_kernel,
        out_shape=jax.ShapeDtypeStruct((N_BA, FL, BLOCK), BF16),
        in_specs=whole(2),
        out_specs=whole(1)[0],
        scratch_shapes=band_scratch(),
        compiler_params=params(24),
        cost_estimate=pl.CostEstimate(
            flops=2 * 14 * FL * 1920 * 128, bytes_accessed=4000000, transcendentals=0
        ),
        name="depart_inner",
    )(targets, grid)


def depart_edges(inner, targets, beside, grid):
    return pl.pallas_call(
        edge_kernel,
        grid=(1,),
        out_shape=jax.ShapeDtypeStruct((N_BA, FL, BLOCK), BF16),
        in_specs=[pl.BlockSpec(memory_space=pl.ANY)] + whole(3),
        out_specs=pl.BlockSpec((2, FL, BLOCK), lambda e: (0, 0, 0)),
        scratch_shapes=band_scratch(),
        input_output_aliases={0: 0},
        compiler_params=params(24),
        name="depart_edges",
    )(inner, targets, beside, grid)


def depart_targets(lat_shift, lon_shift, first_row):
    x = jnp.arange(BLOCK, dtype=jnp.int32) % 128
    centre = (x + lon_shift).astype(F32) + (HALO - 1 + 1.5 - 96)
    sources = first_row + jnp.arange(N_BA, dtype=jnp.int32)[:, None] + lat_shift
    inside = jnp.logical_and(sources >= 0, sources < N_AA * N_BA)
    centre = jnp.where(inside, centre, FAR)
    targets = jnp.stack([jnp.where(lat_shift == s, centre, FAR) for s in (-1, 0, 1)], axis=1)
    return jnp.pad(targets, ((0, 0), (0, 0), (0, WINDOW - BLOCK)), constant_values=FAR)


def wave_places(slot_pairs):
    places = slot_pairs.reshape(N_AA, 1, PAIRS) + (jnp.arange(2) * (WAVES // 2))[None, :, None]
    return places.reshape(1, WAVES).astype(jnp.int32)


def local(legendre, spectral, slot_pairs, lat_shift, lon_shift):
    first = lax.axis_index("aa") * PAIRS
    own = lax.axis_index("ba")
    pairs = jnp.stack([slot_pairs[first + own], slot_pairs[first + N_BA + own // 4]])
    rows = lax.all_to_all(pack(legendre, spectral), "ba", 0, 0, tiled=True)
    sums = lax.all_to_all(legendre_sums(pairs, rows), "ba", 0, 0, tiled=True)
    by_row = regroup(regroup_rows(own), sums)
    coefficients = lax.all_to_all(by_row, "aa", 0, 0, tiled=True)
    blocks = synthesize(wave_places(slot_pairs), coefficients)
    grid = lax.all_to_all(blocks, "ba", 0, 0, tiled=True)
    ends = jnp.stack([grid[N_BA - 1], grid[0]])
    beside = lax.ppermute(ends, "aa", [(i, (i + 1) % N_AA) for i in range(N_AA)])
    targets = depart_targets(lat_shift, lon_shift, lax.axis_index("aa") * N_BA)
    inner = depart_inner(targets, grid)
    return depart_edges(inner, targets, beside, grid)


def solution(mesh):
    placed = (
        P("aa", None, "ba", None, None),
        P("aa", None, None, "ba"),
        P(),
        P("aa", "ba"),
        P("aa", "ba"),
    )
    return jax.shard_map(
        local, mesh=mesh, in_specs=placed, out_specs=P("aa", None, "ba"), check_vma=False
    )
```

```python
import math

import jax
import jax.numpy as jnp
import numpy as np
from jax import lax
from jax.experimental import pallas as pl
from jax.experimental.pallas import tpu as pltpu
from jax.sharding import PartitionSpec as P

WAVES = 1280
NLON = 5120
FL = 64
KPACK = 1281
KTILES = 10
TILES = 7 * KTILES + 1
N_AA = 32
N_BA = 16
PAIRS = 20
HALO = 32
QUARTER = NLON // 4
BLOCK = NLON // N_BA
WINDOW = BLOCK + 2 * HALO
BF16 = jnp.bfloat16
F32 = jnp.float32
NT = (((1,), (1,)), ((), ()))
FAR = -1000.0


def params(mib):
    return pltpu.CompilerParams(vmem_limit_bytes=mib * 1024 * 1024)


def whole(count):
    return [pl.BlockSpec(memory_space=pltpu.VMEM)] * count


def wave_order():
    pairs = np.arange(WAVES // 2)
    return np.concatenate([pairs, WAVES - 1 - pairs])


def window_table():
    starts = np.arange(2)[:, None] * BLOCK - HALO
    lons = (starts + np.arange(WINDOW)[None, :]).reshape(-1)
    phases = wave_order()[:, None] * lons[None, :] % NLON
    angles = phases.astype(np.float32) * np.float32(2.0 * math.pi / NLON)
    factor = np.float32(1.0 / math.sqrt(WAVES))
    table = np.stack([np.cos(angles) * factor, -np.sin(angles) * factor], axis=0)
    return table.astype(np.float32).astype(BF16)


def pack_kernel(rows_ref, values_ref, out_ref, rows_held, values_held, out_held, sems):
    into = [pltpu.make_async_copy(values_ref, values_held, sems.at[PAIRS])]
    for pair in [i for q in range(4) for i in (N_BA + q, 4 * q, 4 * q + 1, 4 * q + 2, 4 * q + 3)]:
        into.append(pltpu.make_async_copy(rows_ref.at[pair], rows_held.at[pair], sems.at[pair]))
    for copy in into:
        copy.start()
    into[0].wait()
    out = []
    lane = lax.broadcasted_iota(jnp.int32, (8, 128), 1)
    for d in range(N_BA):
        q, h = d // 4, d % 4
        if h == 0:
            into[1 + 5 * q].wait()
        into[2 + 5 * q + h].wait()
        last = jnp.zeros((8, 128), F32)
        for g in range(7):
            for k in range(KTILES + 1):
                here = slice(128 * k, min(128 * k + 128, KPACK))
                if g < 4:
                    tile = rows_held[d, 8 * g : 8 * g + 8, here]
                elif g == 4:
                    tile = rows_held[N_BA + q, 8 * h : 8 * h + 8, here]
                else:
                    pair = (d, N_BA + q)[g - 5]
                    tile = values_held[pair, :, :, here].reshape(8, here.stop - here.start)
                if k < KTILES:
                    out_held[d, 7 * k + g] = tile
                else:
                    column = jnp.broadcast_to(tile.astype(F32), (8, 128))
                    last = jnp.where(lane == g, column, last)
        out_held[d, TILES - 1] = last.astype(BF16)
        out.append(pltpu.make_async_copy(out_held.at[d], out_ref.at[d], sems.at[PAIRS + 1 + d]))
        out[-1].start()
    for copy in out:
        copy.wait()


def legendre_kernel(pairs_ref, rows_ref, out_ref):
    column = lax.broadcasted_iota(jnp.int32, (1, 128 * KTILES), 1)
    lane = lax.broadcasted_iota(jnp.int32, (1, 128), 1)
    last = rows_ref[:, TILES - 1]
    for which, (first, count, value) in enumerate(((0, 4, 5), (4, 1, 6))):
        total = N_BA * 8 * count
        left = [
            rows_ref[:, 7 * k + first : 7 * k + first + count].reshape(total, 128)
            for k in range(KTILES)
        ]
        ends = [last * (lane == first + g).astype(F32).astype(BF16) for g in range(count)]
        left.append(jnp.stack(ends, axis=1).reshape(total, 128))
        values = [rows_ref[:, 7 * k + value].reshape(128, 128) for k in range(KTILES)]
        values = jnp.concatenate(values, axis=1)
        end = last.reshape(128, 128)[:, value : value + 1].astype(F32)
        end = jnp.broadcast_to(end, (128, 128)).astype(BF16)
        lower = (column < WAVES - pairs_ref[which]).astype(F32)
        right = jnp.concatenate(
            [
                jnp.concatenate([values * lower.astype(BF16), jnp.zeros_like(end)], axis=1),
                jnp.concatenate([values * (1.0 - lower).astype(BF16), end], axis=1),
            ],
            axis=0,
        )
        left = jnp.concatenate(left, axis=1)
        out = lax.dot_general(left, right, NT, preferred_element_type=F32).astype(BF16)
        out_ref[:, 8 * first : 8 * (first + count), :] = out.reshape(N_BA, 8 * count, 256)


def regroup_rows_kernel(own_ref, out_ref):
    row = iota((WAVES, 1), 0)
    lat = (row // 40 + jnp.where(own_ref[0] == 0, 1, 0)) % N_AA
    pair = row % PAIRS
    shared = (4 * (pair - N_BA) + lat // 8) * 40 + 32 + lat % 8
    source = jnp.where(pair < N_BA, pair * 40 + lat, shared)
    out_ref[...] = ones_where(iota((WAVES, N_BA * 40), 1) == source)


def regroup_kernel(perm_ref, sums_ref, out_ref):
    sums = sums_ref[...].reshape(N_BA * 40, 256)
    both = jnp.dot(perm_ref[...], sums, preferred_element_type=F32)
    first = iota((WAVES, 128), 0) // PAIRS % 2 == 0
    out = jnp.where(first, both[:, :128], both[:, 128:]).astype(BF16)
    out_ref[...] = out.reshape(N_AA, 40, 128)


def iota(shape, dim):
    return lax.broadcasted_iota(jnp.int32, shape, dim)


def ones_where(chosen):
    return chosen.astype(F32).astype(BF16)


def synthesis_kernel(
    places_ref, coef_ref, table_ref, out_ref, rows_ref, left_ref, held_ref, blocks_ref, sems
):
    arriving = pltpu.make_async_copy(coef_ref, rows_ref, sems.at[2 + N_BA])
    arriving.start()
    copies = [
        pltpu.make_async_copy(table_ref.at[c], held_ref.at[c], sems.at[c]) for c in range(2)
    ]
    for copy in copies:
        copy.start()
    row, lane = iota((128, 128), 0), iota((128, 128), 1)
    fields = ones_where(lane == (row % FL) // 4 * 8 + row // FL * 4 + row % 4)
    chosen = ones_where(iota((WAVES, WAVES), 0) == places_ref[...])
    arriving.wait()
    rows = rows_ref[...].reshape(WAVES, 128)
    turned = lax.dot_general(fields, rows, NT, preferred_element_type=F32).astype(BF16)
    ordered = lax.dot_general(turned, chosen, NT, preferred_element_type=F32)
    real, imag = ordered[:FL], ordered[FL:]
    place = iota((1, WAVES), 1)
    wave = jnp.where(place < WAVES // 2, place, WAVES + WAVES // 2 - 1 - place)
    for q in range(4):
        turn = wave * q % 4
        alpha = (turn == 0).astype(F32) - (turn == 2).astype(F32)
        beta = (turn == 1).astype(F32) - (turn == 3).astype(F32)
        here = pl.ds(q * FL, FL)
        left_ref[0, here, :] = (real * alpha - imag * beta).astype(BF16)
        left_ref[1, here, :] = (imag * alpha + real * beta).astype(BF16)
    copies[0].wait()
    even = jnp.dot(left_ref[0], held_ref[0], preferred_element_type=F32)
    copies[1].wait()
    odd = jnp.dot(left_ref[1], held_ref[1], preferred_element_type=F32)
    ahead, behind = (even + odd).astype(BF16), (even - odd).astype(BF16)
    mirror = ones_where(iota((WINDOW, WINDOW), 0) + iota((WINDOW, WINDOW), 1) == WINDOW)
    sent = []

    def finish(block, value):
        blocks_ref[block] = value
        sent.append(pltpu.make_async_copy(blocks_ref.at[block], out_ref.at[block], sems.at[2 + block]))
        sent[-1].start()

    for w in range(2):
        lanes = slice(w * WINDOW, (w + 1) * WINDOW)
        back = jnp.dot(behind[:, lanes], mirror, preferred_element_type=F32).astype(BF16)
        for q in range(4):
            here = slice(q * FL, (q + 1) * FL)
            finish(4 * q + w, ahead[here, lanes])
            finish((4 * q + N_BA - 1 - w) % N_BA, back[here])
    for copy in sent:
        copy.wait()


def band(target, first, count):
    offset = lax.broadcasted_iota(jnp.int32, (count, 128), 0) + (first - 96)
    distance = jnp.abs(offset.astype(F32).astype(BF16) - target.astype(BF16))
    inner = 0.875 - 0.625 * distance
    outer = jnp.minimum(0.0625 * distance - 0.15625, 0.0)
    return jnp.maximum(inner, outer).astype(BF16)


def clear(bands):
    for held in bands:
        held[...] = jnp.zeros_like(held)


def depart_row(target_ref, at, sources, bands, out_ref, to):
    for t, (part, lanes, last, first) in enumerate(((0, 384, 176, 0), (0, 384, 176, 128), (1, 128, 112, 0))):
        for step in range(3):
            target = target_ref[at, step : step + 1, t * 128 : (t + 1) * 128]
            target = jnp.broadcast_to(target, (last - 16, 128))
            begin = step * lanes + first + 16
            bands[part][begin : begin + last - 16, first : first + 128] = band(target, 16, last - 16)
    for part, (lane, x, width) in enumerate(((0, 0, 256), (256, 256, 64))):
        left = jnp.concatenate([s[:, lane:] for s in sources], axis=1)
        out = jnp.dot(left, bands[part][...], preferred_element_type=F32).astype(BF16)
        out_ref[to, :, x : x + width] = out[:, :width]


def inner_kernel(target_ref, grid_ref, out_ref, *bands):
    clear(bands)

    @pl.loop(2, N_BA, unroll=7)
    def _(row):
        above = jnp.where(row == N_BA - 1, 0, row + 1)
        sources = [grid_ref.at[row - 1], grid_ref.at[row], grid_ref.at[above]]
        depart_row(target_ref, row, sources, bands, out_ref, row)


def edge_kernel(inner_ref, target_ref, beside_ref, grid_ref, out_ref, *bands):
    clear(bands)
    sources = [beside_ref.at[0], beside_ref.at[1], grid_ref.at[1], grid_ref.at[2]]
    for row in range(2):
        depart_row(target_ref, row, sources[row : row + 3], bands, out_ref, row)


def pack(legendre, spectral):
    rows = legendre.reshape(PAIRS, N_AA, KPACK)
    values = spectral.transpose(0, 2, 3, 1)
    anywhere = pl.BlockSpec(memory_space=pl.ANY)
    return pl.pallas_call(
        pack_kernel,
        out_shape=jax.ShapeDtypeStruct((N_BA, TILES, 8, 128), BF16),
        in_specs=[anywhere, anywhere],
        out_specs=anywhere,
        scratch_shapes=[
            pltpu.VMEM((PAIRS, N_AA, KPACK), BF16),
            pltpu.VMEM((PAIRS, 2, 4, KPACK), BF16),
            pltpu.VMEM((N_BA, TILES, 8, 128), BF16),
            pltpu.SemaphoreType.DMA((PAIRS + 1 + N_BA,)),
        ],
        compiler_params=params(59),
        name="pack",
    )(rows, values)


def legendre_sums(pairs, rows):
    return pl.pallas_call(
        legendre_kernel,
        out_shape=jax.ShapeDtypeStruct((N_BA, 40, 256), BF16),
        in_specs=[pl.BlockSpec(memory_space=pltpu.SMEM)] + whole(1),
        out_specs=whole(1)[0],
        compiler_params=params(24),
        name="legendre_sums",
    )(pairs, rows)


def regroup(perm, sums):
    return pl.pallas_call(
        regroup_kernel,
        out_shape=jax.ShapeDtypeStruct((N_AA, 40, 128), BF16),
        in_specs=whole(2),
        out_specs=whole(1)[0],
        compiler_params=params(24),
        name="regroup",
    )(perm, sums)


def regroup_rows(own):
    return pl.pallas_call(
        regroup_rows_kernel,
        out_shape=jax.ShapeDtypeStruct((WAVES, N_BA * 40), BF16),
        in_specs=[pl.BlockSpec(memory_space=pltpu.SMEM)],
        out_specs=whole(1)[0],
        compiler_params=params(8),
        name="regroup_rows",
    )(own.reshape(1).astype(jnp.int32))


def synthesize(places, coefficients):
    anywhere = pl.BlockSpec(memory_space=pl.ANY)
    return pl.pallas_call(
        synthesis_kernel,
        out_shape=jax.ShapeDtypeStruct((N_BA, FL, WINDOW), BF16),
        in_specs=whole(1) + [anywhere] * 2,
        out_specs=anywhere,
        scratch_shapes=[
            pltpu.VMEM((N_AA, 40, 128), BF16),
            pltpu.VMEM((2, 4 * FL, WAVES), BF16),
            pltpu.VMEM((2, WAVES, 2 * WINDOW), BF16),
            pltpu.VMEM((N_BA, FL, WINDOW), BF16),
            pltpu.SemaphoreType.DMA((3 + N_BA,)),
        ],
        compiler_params=params(50),
        name="synthesize",
    )(places, coefficients, jnp.asarray(window_table()))


def band_scratch():
    return [pltpu.VMEM((1152, 256), BF16), pltpu.VMEM((384, 128), BF16)]


def depart_inner(targets, grid):
    return pl.pallas_call(
        inner_kernel,
        out_shape=jax.ShapeDtypeStruct((N_BA, FL, BLOCK), BF16),
        in_specs=whole(2),
        out_specs=whole(1)[0],
        scratch_shapes=band_scratch(),
        compiler_params=params(24),
        cost_estimate=pl.CostEstimate(
            flops=2 * 14 * FL * 1920 * 128, bytes_accessed=4000000, transcendentals=0
        ),
        name="depart_inner",
    )(targets, grid)


def depart_edges(inner, targets, beside, grid):
    return pl.pallas_call(
        edge_kernel,
        grid=(1,),
        out_shape=jax.ShapeDtypeStruct((N_BA, FL, BLOCK), BF16),
        in_specs=[pl.BlockSpec(memory_space=pl.ANY)] + whole(3),
        out_specs=pl.BlockSpec((2, FL, BLOCK), lambda e: (0, 0, 0)),
        scratch_shapes=band_scratch(),
        input_output_aliases={0: 0},
        compiler_params=params(24),
        name="depart_edges",
    )(inner, targets, beside, grid)


def depart_targets(lat_shift, lon_shift, first_row):
    x = jnp.arange(BLOCK, dtype=jnp.int32) % 128
    centre = (x + lon_shift).astype(F32) + (HALO - 1 + 1.5 - 96)
    sources = first_row + jnp.arange(N_BA, dtype=jnp.int32)[:, None] + lat_shift
    inside = jnp.logical_and(sources >= 0, sources < N_AA * N_BA)
    centre = jnp.where(inside, centre, FAR)
    targets = jnp.stack([jnp.where(lat_shift == s, centre, FAR) for s in (-1, 0, 1)], axis=1)
    return jnp.pad(targets, ((0, 0), (0, 0), (0, WINDOW - BLOCK)), constant_values=FAR)


def wave_places(slot_pairs):
    places = slot_pairs.reshape(N_AA, 1, PAIRS) + (jnp.arange(2) * (WAVES // 2))[None, :, None]
    return places.reshape(1, WAVES).astype(jnp.int32)


def local(legendre, spectral, slot_pairs, lat_shift, lon_shift):
    first = lax.axis_index("aa") * PAIRS
    own = lax.axis_index("ba")
    pairs = jnp.stack([slot_pairs[first + own], slot_pairs[first + N_BA + own // 4]])
    rows = lax.all_to_all(pack(legendre, spectral), "ba", 0, 0, tiled=True)
    pairs, perm = lax.optimization_barrier((pairs, regroup_rows(own)))
    sums = lax.all_to_all(legendre_sums(pairs, rows), "ba", 0, 0, tiled=True)
    by_row = regroup(perm, sums)
    coefficients = lax.all_to_all(by_row, "aa", 0, 0, tiled=True)
    blocks = synthesize(wave_places(slot_pairs), coefficients)
    grid = lax.all_to_all(blocks, "ba", 0, 0, tiled=True)
    ends = jnp.stack([grid[N_BA - 1], grid[0]])
    beside = lax.ppermute(ends, "aa", [(i, (i + 1) % N_AA) for i in range(N_AA)])
    targets = depart_targets(lat_shift, lon_shift, lax.axis_index("aa") * N_BA)
    inner = depart_inner(targets, grid)
    return depart_edges(inner, targets, beside, grid)


def solution(mesh):
    placed = (
        P("aa", None, "ba", None, None),
        P("aa", None, None, "ba"),
        P(),
        P("aa", "ba"),
        P("aa", "ba"),
    )
    return jax.shard_map(
        local, mesh=mesh, in_specs=placed, out_specs=P("aa", None, "ba"), check_vma=False
    )
```

```python
import math

import jax
import jax.numpy as jnp
import numpy as np
from jax import lax
from jax.experimental import pallas as pl
from jax.experimental.pallas import tpu as pltpu
from jax.sharding import PartitionSpec as P

WAVES = 1280
NLON = 5120
FL = 64
KPACK = 1281
KTILES = 10
TILES = 7 * KTILES + 1
N_AA = 32
N_BA = 16
PAIRS = 20
HALO = 32
QUARTER = NLON // 4
BLOCK = NLON // N_BA
WINDOW = BLOCK + 2 * HALO
BF16 = jnp.bfloat16
F32 = jnp.float32
NT = (((1,), (1,)), ((), ()))
FAR = -1000.0


def params(mib):
    return pltpu.CompilerParams(vmem_limit_bytes=mib * 1024 * 1024)


def whole(count):
    return [pl.BlockSpec(memory_space=pltpu.VMEM)] * count


def wave_order():
    pairs = np.arange(WAVES // 2)
    return np.concatenate([pairs, WAVES - 1 - pairs])


def window_table():
    starts = np.arange(2)[:, None] * BLOCK - HALO
    lons = (starts + np.arange(WINDOW)[None, :]).reshape(-1)
    phases = wave_order()[:, None] * lons[None, :] % NLON
    angles = phases.astype(np.float32) * np.float32(2.0 * math.pi / NLON)
    factor = np.float32(1.0 / math.sqrt(WAVES))
    table = np.stack([np.cos(angles) * factor, -np.sin(angles) * factor], axis=0)
    return table.astype(np.float32).astype(BF16)


def pack_kernel(rows_ref, values_ref, out_ref, rows_held, values_held, out_held, sems):
    into = [pltpu.make_async_copy(values_ref, values_held, sems.at[PAIRS])]
    for pair in [i for q in range(4) for i in (N_BA + q, 4 * q, 4 * q + 1, 4 * q + 2, 4 * q + 3)]:
        into.append(pltpu.make_async_copy(rows_ref.at[pair], rows_held.at[pair], sems.at[pair]))
    for copy in into:
        copy.start()
    into[0].wait()
    out = []
    lane = lax.broadcasted_iota(jnp.int32, (8, 128), 1)
    for d in range(N_BA):
        q, h = d // 4, d % 4
        if h == 0:
            into[1 + 5 * q].wait()
        into[2 + 5 * q + h].wait()
        last = jnp.zeros((8, 128), F32)
        for g in range(7):
            for k in range(KTILES + 1):
                here = slice(128 * k, min(128 * k + 128, KPACK))
                if g < 4:
                    tile = rows_held[d, 8 * g : 8 * g + 8, here]
                elif g == 4:
                    tile = rows_held[N_BA + q, 8 * h : 8 * h + 8, here]
                else:
                    pair = (d, N_BA + q)[g - 5]
                    tile = values_held[pair, :, :, here].reshape(8, here.stop - here.start)
                if k < KTILES:
                    out_held[d, 7 * k + g] = tile
                else:
                    column = jnp.broadcast_to(tile.astype(F32), (8, 128))
                    last = jnp.where(lane == g, column, last)
        out_held[d, TILES - 1] = last.astype(BF16)
        out.append(pltpu.make_async_copy(out_held.at[d], out_ref.at[d], sems.at[PAIRS + 1 + d]))
        out[-1].start()
    for copy in out:
        copy.wait()


def legendre_kernel(pairs_ref, rows_ref, out_ref):
    column = lax.broadcasted_iota(jnp.int32, (1, 128 * KTILES), 1)
    lane = lax.broadcasted_iota(jnp.int32, (1, 128), 1)
    last = rows_ref[:, TILES - 1]
    for which, (first, count, value) in enumerate(((0, 4, 5), (4, 1, 6))):
        total = N_BA * 8 * count
        left = [
            rows_ref[:, 7 * k + first : 7 * k + first + count].reshape(total, 128)
            for k in range(KTILES)
        ]
        ends = [last * (lane == first + g).astype(F32).astype(BF16) for g in range(count)]
        left.append(jnp.stack(ends, axis=1).reshape(total, 128))
        values = [rows_ref[:, 7 * k + value].reshape(128, 128) for k in range(KTILES)]
        values = jnp.concatenate(values, axis=1)
        end = last.reshape(128, 128)[:, value : value + 1].astype(F32)
        end = jnp.broadcast_to(end, (128, 128)).astype(BF16)
        lower = (column < WAVES - pairs_ref[which]).astype(F32)
        right = jnp.concatenate(
            [
                jnp.concatenate([values * lower.astype(BF16), jnp.zeros_like(end)], axis=1),
                jnp.concatenate([values * (1.0 - lower).astype(BF16), end], axis=1),
            ],
            axis=0,
        )
        left = jnp.concatenate(left, axis=1)
        out = lax.dot_general(left, right, NT, preferred_element_type=F32).astype(BF16)
        out_ref[:, 8 * first : 8 * (first + count), :] = out.reshape(N_BA, 8 * count, 256)


def regroup_rows_kernel(own_ref, out_ref):
    row = iota((WAVES, 1), 0)
    lat = (row // 40 + jnp.where(own_ref[0] == 0, 1, 0)) % N_AA
    pair = row % PAIRS
    shared = (4 * (pair - N_BA) + lat // 8) * 40 + 32 + lat % 8
    source = jnp.where(pair < N_BA, pair * 40 + lat, shared)
    out_ref[...] = ones_where(iota((WAVES, N_BA * 40), 1) == source)


def regroup_kernel(perm_ref, sums_ref, out_ref):
    sums = sums_ref[...].reshape(N_BA * 40, 256)
    both = jnp.dot(perm_ref[...], sums, preferred_element_type=F32)
    first = iota((WAVES, 128), 0) // PAIRS % 2 == 0
    out = jnp.where(first, both[:, :128], both[:, 128:]).astype(BF16)
    out_ref[...] = out.reshape(N_AA, 40, 128)


def iota(shape, dim):
    return lax.broadcasted_iota(jnp.int32, shape, dim)


def ones_where(chosen):
    return chosen.astype(F32).astype(BF16)


def synthesis_kernel(places_ref, coef_ref, table_ref, out_ref, left_ref):
    row, lane = iota((128, 128), 0), iota((128, 128), 1)
    fields = ones_where(lane == (row % FL) // 4 * 8 + row // FL * 4 + row % 4)
    chosen = ones_where(iota((WAVES, WAVES), 0) == places_ref[...])
    rows = coef_ref[...].reshape(WAVES, 128)
    turned = lax.dot_general(fields, rows, NT, preferred_element_type=F32).astype(BF16)
    ordered = lax.dot_general(turned, chosen, NT, preferred_element_type=F32)
    real, imag = ordered[:FL], ordered[FL:]
    place = iota((1, WAVES), 1)
    wave = jnp.where(place < WAVES // 2, place, WAVES + WAVES // 2 - 1 - place)
    for q in range(4):
        turn = wave * q % 4
        alpha = (turn == 0).astype(F32) - (turn == 2).astype(F32)
        beta = (turn == 1).astype(F32) - (turn == 3).astype(F32)
        here = pl.ds(q * FL, FL)
        left_ref[0, here, :] = (real * alpha - imag * beta).astype(BF16)
        left_ref[1, here, :] = (imag * alpha + real * beta).astype(BF16)
    even = jnp.dot(left_ref[0], table_ref[0], preferred_element_type=F32)
    odd = jnp.dot(left_ref[1], table_ref[1], preferred_element_type=F32)
    ahead, behind = (even + odd).astype(BF16), (even - odd).astype(BF16)
    mirror = ones_where(iota((WINDOW, WINDOW), 0) + iota((WINDOW, WINDOW), 1) == WINDOW)
    for w in range(2):
        lanes = slice(w * WINDOW, (w + 1) * WINDOW)
        back = jnp.dot(behind[:, lanes], mirror, preferred_element_type=F32).astype(BF16)
        for q in range(4):
            here = slice(q * FL, (q + 1) * FL)
            out_ref[4 * q + w] = ahead[here, lanes]
            out_ref[(4 * q + N_BA - 1 - w) % N_BA] = back[here]


def band(target, first, count):
    offset = lax.broadcasted_iota(jnp.int32, (count, 128), 0) + (first - 96)
    distance = jnp.abs(offset.astype(F32).astype(BF16) - target.astype(BF16))
    inner = 0.875 - 0.625 * distance
    outer = jnp.minimum(0.0625 * distance - 0.15625, 0.0)
    return jnp.maximum(inner, outer).astype(BF16)


def clear(bands):
    for held in bands:
        held[...] = jnp.zeros_like(held)


def depart_row(target_ref, at, sources, bands, out_ref, to):
    for t, (part, lanes, last, first) in enumerate(((0, 384, 176, 0), (0, 384, 176, 128), (1, 128, 112, 0))):
        for step in range(3):
            target = target_ref[at, step : step + 1, t * 128 : (t + 1) * 128]
            target = jnp.broadcast_to(target, (last - 16, 128))
            begin = step * lanes + first + 16
            bands[part][begin : begin + last - 16, first : first + 128] = band(target, 16, last - 16)
    for part, (lane, x, width) in enumerate(((0, 0, 256), (256, 256, 64))):
        left = jnp.concatenate([s[:, lane:] for s in sources], axis=1)
        out = jnp.dot(left, bands[part][...], preferred_element_type=F32).astype(BF16)
        out_ref[to, :, x : x + width] = out[:, :width]


def inner_kernel(target_ref, grid_ref, out_ref, *bands):
    clear(bands)

    @pl.loop(2, N_BA, unroll=7)
    def _(row):
        above = jnp.where(row == N_BA - 1, 0, row + 1)
        sources = [grid_ref.at[row - 1], grid_ref.at[row], grid_ref.at[above]]
        depart_row(target_ref, row, sources, bands, out_ref, row)


def edge_kernel(inner_ref, target_ref, beside_ref, grid_ref, out_ref, *bands):
    clear(bands)
    sources = [beside_ref.at[0], beside_ref.at[1], grid_ref.at[1], grid_ref.at[2]]
    for row in range(2):
        depart_row(target_ref, row, sources[row : row + 3], bands, out_ref, row)


def pack(legendre, spectral):
    rows = legendre.reshape(PAIRS, N_AA, KPACK)
    values = spectral.transpose(0, 2, 3, 1)
    anywhere = pl.BlockSpec(memory_space=pl.ANY)
    return pl.pallas_call(
        pack_kernel,
        out_shape=jax.ShapeDtypeStruct((N_BA, TILES, 8, 128), BF16),
        in_specs=[anywhere, anywhere],
        out_specs=anywhere,
        scratch_shapes=[
            pltpu.VMEM((PAIRS, N_AA, KPACK), BF16),
            pltpu.VMEM((PAIRS, 2, 4, KPACK), BF16),
            pltpu.VMEM((N_BA, TILES, 8, 128), BF16),
            pltpu.SemaphoreType.DMA((PAIRS + 1 + N_BA,)),
        ],
        compiler_params=params(59),
        name="pack",
    )(rows, values)


def legendre_sums(pairs, rows):
    return pl.pallas_call(
        legendre_kernel,
        out_shape=jax.ShapeDtypeStruct((N_BA, 40, 256), BF16),
        in_specs=[pl.BlockSpec(memory_space=pltpu.SMEM)] + whole(1),
        out_specs=whole(1)[0],
        compiler_params=params(24),
        name="legendre_sums",
    )(pairs, rows)


def regroup(perm, sums):
    return pl.pallas_call(
        regroup_kernel,
        out_shape=jax.ShapeDtypeStruct((N_AA, 40, 128), BF16),
        in_specs=whole(2),
        out_specs=whole(1)[0],
        compiler_params=params(24),
        name="regroup",
    )(perm, sums)


def regroup_rows(own):
    return pl.pallas_call(
        regroup_rows_kernel,
        out_shape=jax.ShapeDtypeStruct((WAVES, N_BA * 40), BF16),
        in_specs=[pl.BlockSpec(memory_space=pltpu.SMEM)],
        out_specs=whole(1)[0],
        compiler_params=params(8),
        name="regroup_rows",
    )(own.reshape(1).astype(jnp.int32))


def synthesize(places, coefficients):
    return pl.pallas_call(
        synthesis_kernel,
        out_shape=jax.ShapeDtypeStruct((N_BA, FL, WINDOW), BF16),
        in_specs=whole(3),
        out_specs=whole(1)[0],
        scratch_shapes=[pltpu.VMEM((2, 4 * FL, WAVES), BF16)],
        compiler_params=params(24),
        name="synthesize",
    )(places, coefficients, jnp.asarray(window_table()))


def band_scratch():
    return [pltpu.VMEM((1152, 256), BF16), pltpu.VMEM((384, 128), BF16)]


def depart_inner(targets, grid):
    return pl.pallas_call(
        inner_kernel,
        out_shape=jax.ShapeDtypeStruct((N_BA, FL, BLOCK), BF16),
        in_specs=whole(2),
        out_specs=whole(1)[0],
        scratch_shapes=band_scratch(),
        compiler_params=params(24),
        cost_estimate=pl.CostEstimate(
            flops=2 * 14 * FL * 1920 * 128, bytes_accessed=4000000, transcendentals=0
        ),
        name="depart_inner",
    )(targets, grid)


def depart_edges(inner, targets, beside, grid):
    return pl.pallas_call(
        edge_kernel,
        grid=(1,),
        out_shape=jax.ShapeDtypeStruct((N_BA, FL, BLOCK), BF16),
        in_specs=[pl.BlockSpec(memory_space=pl.ANY)] + whole(3),
        out_specs=pl.BlockSpec((2, FL, BLOCK), lambda e: (0, 0, 0)),
        scratch_shapes=band_scratch(),
        input_output_aliases={0: 0},
        compiler_params=params(24),
        name="depart_edges",
    )(inner, targets, beside, grid)


def depart_targets(lat_shift, lon_shift, first_row):
    x = jnp.arange(BLOCK, dtype=jnp.int32) % 128
    centre = (x + lon_shift).astype(F32) + (HALO - 1 + 1.5 - 96)
    sources = first_row + jnp.arange(N_BA, dtype=jnp.int32)[:, None] + lat_shift
    inside = jnp.logical_and(sources >= 0, sources < N_AA * N_BA)
    centre = jnp.where(inside, centre, FAR)
    targets = jnp.stack([jnp.where(lat_shift == s, centre, FAR) for s in (-1, 0, 1)], axis=1)
    return jnp.pad(targets, ((0, 0), (0, 0), (0, WINDOW - BLOCK)), constant_values=FAR)


def wave_places(slot_pairs):
    places = slot_pairs.reshape(N_AA, 1, PAIRS) + (jnp.arange(2) * (WAVES // 2))[None, :, None]
    return places.reshape(1, WAVES).astype(jnp.int32)


def local(legendre, spectral, slot_pairs, lat_shift, lon_shift):
    first = lax.axis_index("aa") * PAIRS
    own = lax.axis_index("ba")
    pairs = jnp.stack([slot_pairs[first + own], slot_pairs[first + N_BA + own // 4]])
    rows = lax.all_to_all(pack(legendre, spectral), "ba", 0, 0, tiled=True)
    targets = depart_targets(lat_shift, lon_shift, lax.axis_index("aa") * N_BA)
    pairs, perm, places, targets = lax.optimization_barrier(
        (pairs, regroup_rows(own), wave_places(slot_pairs), targets)
    )
    sums = lax.all_to_all(legendre_sums(pairs, rows), "ba", 0, 0, tiled=True)
    by_row = regroup(perm, sums)
    coefficients = lax.all_to_all(by_row, "aa", 0, 0, tiled=True)
    blocks = synthesize(places, coefficients)
    grid = lax.all_to_all(blocks, "ba", 0, 0, tiled=True)
    ends = jnp.stack([grid[N_BA - 1], grid[0]])
    beside = lax.ppermute(ends, "aa", [(i, (i + 1) % N_AA) for i in range(N_AA)])
    inner = depart_inner(targets, grid)
    return depart_edges(inner, targets, beside, grid)


def solution(mesh):
    placed = (
        P("aa", None, "ba", None, None),
        P("aa", None, None, "ba"),
        P(),
        P("aa", "ba"),
        P("aa", "ba"),
    )
    return jax.shard_map(
        local, mesh=mesh, in_specs=placed, out_specs=P("aa", None, "ba"), check_vma=False
    )
```

```python
import math

import jax
import jax.numpy as jnp
import numpy as np
from jax import lax
from jax.experimental import pallas as pl
from jax.experimental.pallas import tpu as pltpu
from jax.sharding import PartitionSpec as P

WAVES = 1280
NLON = 5120
FL = 64
KPACK = 1281
KTILES = 10
TILES = 7 * KTILES + 1
N_AA = 32
N_BA = 16
PAIRS = 20
HALO = 32
QUARTER = NLON // 4
BLOCK = NLON // N_BA
WINDOW = BLOCK + 2 * HALO
BF16 = jnp.bfloat16
F32 = jnp.float32
NT = (((1,), (1,)), ((), ()))
FAR = -1000.0


def params(mib):
    return pltpu.CompilerParams(vmem_limit_bytes=mib * 1024 * 1024)


def whole(count):
    return [pl.BlockSpec(memory_space=pltpu.VMEM)] * count


def wave_order():
    pairs = np.arange(WAVES // 2)
    return np.concatenate([pairs, WAVES - 1 - pairs])


def window_table():
    starts = np.arange(2)[:, None] * BLOCK - HALO
    lons = (starts + np.arange(WINDOW)[None, :]).reshape(-1)
    phases = wave_order()[:, None] * lons[None, :] % NLON
    angles = phases.astype(np.float32) * np.float32(2.0 * math.pi / NLON)
    factor = np.float32(1.0 / math.sqrt(WAVES))
    table = np.stack([np.cos(angles) * factor, -np.sin(angles) * factor], axis=0)
    return table.astype(np.float32).astype(BF16)


def pack_kernel(rows_ref, values_ref, out_ref, rows_held, values_held, out_held, sems):
    into = []
    for q in range(4):
        four = pl.ds(4 * q, 4)
        into.append(
            [
                pltpu.make_async_copy(rows_ref.at[N_BA + q], rows_held.at[N_BA + q], sems.at[q]),
                pltpu.make_async_copy(values_ref.at[N_BA + q], values_held.at[N_BA + q], sems.at[4 + q]),
                pltpu.make_async_copy(rows_ref.at[four], rows_held.at[four], sems.at[8 + q]),
                pltpu.make_async_copy(values_ref.at[four], values_held.at[four], sems.at[12 + q]),
            ]
        )
        for copy in into[q]:
            copy.start()
    out = []
    lane = lax.broadcasted_iota(jnp.int32, (8, 128), 1)
    for d in range(N_BA):
        q, h = d // 4, d % 4
        if h == 0:
            for copy in into[q]:
                copy.wait()
        last = jnp.zeros((8, 128), F32)
        for g in range(7):
            for k in range(KTILES + 1):
                here = slice(128 * k, min(128 * k + 128, KPACK))
                if g < 4:
                    tile = rows_held[d, 8 * g : 8 * g + 8, here]
                elif g == 4:
                    tile = rows_held[N_BA + q, 8 * h : 8 * h + 8, here]
                else:
                    pair = (d, N_BA + q)[g - 5]
                    tile = values_held[pair, :, :, here].reshape(8, here.stop - here.start)
                if k < KTILES:
                    out_held[d, 7 * k + g] = tile
                else:
                    column = jnp.broadcast_to(tile.astype(F32), (8, 128))
                    last = jnp.where(lane == g, column, last)
        out_held[d, TILES - 1] = last.astype(BF16)
        out.append(pltpu.make_async_copy(out_held.at[d], out_ref.at[d], sems.at[PAIRS + 1 + d]))
        out[-1].start()
    for copy in out:
        copy.wait()


def legendre_kernel(pairs_ref, rows_ref, out_ref):
    column = lax.broadcasted_iota(jnp.int32, (1, 128 * KTILES), 1)
    lane = lax.broadcasted_iota(jnp.int32, (1, 128), 1)
    last = rows_ref[:, TILES - 1]
    for which, (first, count, value) in enumerate(((0, 4, 5), (4, 1, 6))):
        total = N_BA * 8 * count
        left = [
            rows_ref[:, 7 * k + first : 7 * k + first + count].reshape(total, 128)
            for k in range(KTILES)
        ]
        ends = [last * (lane == first + g).astype(F32).astype(BF16) for g in range(count)]
        left.append(jnp.stack(ends, axis=1).reshape(total, 128))
        values = [rows_ref[:, 7 * k + value].reshape(128, 128) for k in range(KTILES)]
        values = jnp.concatenate(values, axis=1)
        end = last.reshape(128, 128)[:, value : value + 1].astype(F32)
        end = jnp.broadcast_to(end, (128, 128)).astype(BF16)
        lower = (column < WAVES - pairs_ref[which]).astype(F32)
        right = jnp.concatenate(
            [
                jnp.concatenate([values * lower.astype(BF16), jnp.zeros_like(end)], axis=1),
                jnp.concatenate([values * (1.0 - lower).astype(BF16), end], axis=1),
            ],
            axis=0,
        )
        left = jnp.concatenate(left, axis=1)
        out = lax.dot_general(left, right, NT, preferred_element_type=F32).astype(BF16)
        out_ref[:, 8 * first : 8 * (first + count), :] = out.reshape(N_BA, 8 * count, 256)


def regroup_rows_kernel(own_ref, out_ref):
    row = iota((WAVES, 1), 0)
    lat = (row // 40 + jnp.where(own_ref[0] == 0, 1, 0)) % N_AA
    pair = row % PAIRS
    shared = (4 * (pair - N_BA) + lat // 8) * 40 + 32 + lat % 8
    source = jnp.where(pair < N_BA, pair * 40 + lat, shared)
    out_ref[...] = ones_where(iota((WAVES, N_BA * 40), 1) == source)


def regroup_kernel(perm_ref, sums_ref, out_ref):
    sums = sums_ref[...].reshape(N_BA * 40, 256)
    both = jnp.dot(perm_ref[...], sums, preferred_element_type=F32)
    first = iota((WAVES, 128), 0) // PAIRS % 2 == 0
    out = jnp.where(first, both[:, :128], both[:, 128:]).astype(BF16)
    out_ref[...] = out.reshape(N_AA, 40, 128)


def iota(shape, dim):
    return lax.broadcasted_iota(jnp.int32, shape, dim)


def ones_where(chosen):
    return chosen.astype(F32).astype(BF16)


def synthesis_kernel(places_ref, coef_ref, table_ref, out_ref, left_ref):
    row, lane = iota((128, 128), 0), iota((128, 128), 1)
    fields = ones_where(lane == (row % FL) // 4 * 8 + row // FL * 4 + row % 4)
    chosen = ones_where(iota((WAVES, WAVES), 0) == places_ref[...])
    rows = coef_ref[...].reshape(WAVES, 128)
    turned = lax.dot_general(fields, rows, NT, preferred_element_type=F32).astype(BF16)
    ordered = lax.dot_general(turned, chosen, NT, preferred_element_type=F32)
    real, imag = ordered[:FL], ordered[FL:]
    place = iota((1, WAVES), 1)
    wave = jnp.where(place < WAVES // 2, place, WAVES + WAVES // 2 - 1 - place)
    for q in range(4):
        turn = wave * q % 4
        alpha = (turn == 0).astype(F32) - (turn == 2).astype(F32)
        beta = (turn == 1).astype(F32) - (turn == 3).astype(F32)
        here = pl.ds(q * FL, FL)
        left_ref[0, here, :] = (real * alpha - imag * beta).astype(BF16)
        left_ref[1, here, :] = (imag * alpha + real * beta).astype(BF16)
    even = jnp.dot(left_ref[0], table_ref[0], preferred_element_type=F32)
    odd = jnp.dot(left_ref[1], table_ref[1], preferred_element_type=F32)
    ahead, behind = (even + odd).astype(BF16), (even - odd).astype(BF16)
    mirror = ones_where(iota((WINDOW, WINDOW), 0) + iota((WINDOW, WINDOW), 1) == WINDOW)
    for w in range(2):
        lanes = slice(w * WINDOW, (w + 1) * WINDOW)
        back = jnp.dot(behind[:, lanes], mirror, preferred_element_type=F32).astype(BF16)
        for q in range(4):
            here = slice(q * FL, (q + 1) * FL)
            out_ref[4 * q + w] = ahead[here, lanes]
            out_ref[(4 * q + N_BA - 1 - w) % N_BA] = back[here]


def band(target, first, count):
    offset = lax.broadcasted_iota(jnp.int32, (count, 128), 0) + (first - 96)
    distance = jnp.abs(offset.astype(F32).astype(BF16) - target.astype(BF16))
    inner = 0.875 - 0.625 * distance
    outer = jnp.minimum(0.0625 * distance - 0.15625, 0.0)
    return jnp.maximum(inner, outer).astype(BF16)


def clear(bands):
    for held in bands:
        held[...] = jnp.zeros_like(held)


def fill_bands(target_ref, at, bands):
    for t, (part, lanes, last, first) in enumerate(((0, 384, 176, 0), (0, 384, 176, 128), (1, 128, 112, 0))):
        for step in range(3):
            target = target_ref[at, step : step + 1, t * 128 : (t + 1) * 128]
            target = jnp.broadcast_to(target, (last - 16, 128))
            begin = step * lanes + first + 16
            bands[part][begin : begin + last - 16, first : first + 128] = band(target, 16, last - 16)


def multiply_bands(sources, bands, out_ref, to):
    for part, (lane, x, width) in enumerate(((0, 0, 256), (256, 256, 64))):
        left = jnp.concatenate([s[:, lane:] for s in sources], axis=1)
        out = jnp.dot(left, bands[part][...], preferred_element_type=F32).astype(BF16)
        out_ref[to, :, x : x + width] = out[:, :width]


def inner_kernel(target_ref, grid_ref, out_ref, *bands):
    clear(bands)

    @pl.loop(2, N_BA, unroll=14)
    def _(row):
        above = jnp.where(row == N_BA - 1, 0, row + 1)
        sources = [grid_ref.at[row - 1], grid_ref.at[row], grid_ref.at[above]]
        fill_bands(target_ref, row, bands)
        multiply_bands(sources, bands, out_ref, row)


def edge_bands_kernel(target_ref, *bands):
    clear(bands)
    for row in range(2):
        fill_bands(target_ref, row, [held.at[row] for held in bands])


def edge_kernel(inner_ref, wide_ref, narrow_ref, beside_ref, grid_ref, out_ref):
    sources = [beside_ref.at[0], beside_ref.at[1], grid_ref.at[1], grid_ref.at[2]]
    for row in range(2):
        bands = [wide_ref.at[row], narrow_ref.at[row]]
        multiply_bands(sources[row : row + 3], bands, out_ref, row)


def pack(legendre, spectral):
    rows = legendre.reshape(PAIRS, N_AA, KPACK)
    values = spectral.transpose(0, 2, 3, 1)
    anywhere = pl.BlockSpec(memory_space=pl.ANY)
    return pl.pallas_call(
        pack_kernel,
        out_shape=jax.ShapeDtypeStruct((N_BA, TILES, 8, 128), BF16),
        in_specs=[anywhere, anywhere],
        out_specs=anywhere,
        scratch_shapes=[
            pltpu.VMEM((PAIRS, N_AA, KPACK), BF16),
            pltpu.VMEM((PAIRS, 2, 4, KPACK), BF16),
            pltpu.VMEM((N_BA, TILES, 8, 128), BF16),
            pltpu.SemaphoreType.DMA((PAIRS + 1 + N_BA,)),
        ],
        compiler_params=params(59),
        name="pack",
    )(rows, values)


def legendre_sums(pairs, rows):
    return pl.pallas_call(
        legendre_kernel,
        out_shape=jax.ShapeDtypeStruct((N_BA, 40, 256), BF16),
        in_specs=[pl.BlockSpec(memory_space=pltpu.SMEM)] + whole(1),
        out_specs=whole(1)[0],
        compiler_params=params(24),
        name="legendre_sums",
    )(pairs, rows)


def regroup(perm, sums):
    return pl.pallas_call(
        regroup_kernel,
        out_shape=jax.ShapeDtypeStruct((N_AA, 40, 128), BF16),
        in_specs=whole(2),
        out_specs=whole(1)[0],
        compiler_params=params(24),
        name="regroup",
    )(perm, sums)


def regroup_rows(own):
    return pl.pallas_call(
        regroup_rows_kernel,
        out_shape=jax.ShapeDtypeStruct((WAVES, N_BA * 40), BF16),
        in_specs=[pl.BlockSpec(memory_space=pltpu.SMEM)],
        out_specs=whole(1)[0],
        compiler_params=params(8),
        name="regroup_rows",
    )(own.reshape(1).astype(jnp.int32))


def synthesize(places, coefficients):
    return pl.pallas_call(
        synthesis_kernel,
        out_shape=jax.ShapeDtypeStruct((N_BA, FL, WINDOW), BF16),
        in_specs=whole(3),
        out_specs=whole(1)[0],
        scratch_shapes=[pltpu.VMEM((2, 4 * FL, WAVES), BF16)],
        compiler_params=params(24),
        name="synthesize",
    )(places, coefficients, jnp.asarray(window_table()))


def band_scratch():
    return [pltpu.VMEM((1152, 256), BF16), pltpu.VMEM((384, 128), BF16)]


def depart_inner(targets, grid):
    return pl.pallas_call(
        inner_kernel,
        out_shape=jax.ShapeDtypeStruct((N_BA, FL, BLOCK), BF16),
        in_specs=whole(2),
        out_specs=whole(1)[0],
        scratch_shapes=band_scratch(),
        compiler_params=params(24),
        cost_estimate=pl.CostEstimate(
            flops=2 * 14 * FL * 1920 * 128, bytes_accessed=4000000, transcendentals=0
        ),
        name="depart_inner",
    )(targets, grid)


def edge_bands(targets):
    return pl.pallas_call(
        edge_bands_kernel,
        out_shape=(
            jax.ShapeDtypeStruct((2, 1152, 256), BF16),
            jax.ShapeDtypeStruct((2, 384, 128), BF16),
        ),
        in_specs=whole(1),
        out_specs=tuple(whole(2)),
        compiler_params=params(8),
        name="edge_bands",
    )(targets)


def depart_edges(inner, bands, beside, grid):
    return pl.pallas_call(
        edge_kernel,
        grid=(1,),
        out_shape=jax.ShapeDtypeStruct((N_BA, FL, BLOCK), BF16),
        in_specs=[pl.BlockSpec(memory_space=pl.ANY)] + whole(4),
        out_specs=pl.BlockSpec((2, FL, BLOCK), lambda e: (0, 0, 0)),
        input_output_aliases={0: 0},
        compiler_params=params(24),
        name="depart_edges",
    )(inner, *bands, beside, grid)


def depart_targets(lat_shift, lon_shift, first_row):
    x = jnp.arange(BLOCK, dtype=jnp.int32) % 128
    centre = (x + lon_shift).astype(F32) + (HALO - 1 + 1.5 - 96)
    sources = first_row + jnp.arange(N_BA, dtype=jnp.int32)[:, None] + lat_shift
    inside = jnp.logical_and(sources >= 0, sources < N_AA * N_BA)
    centre = jnp.where(inside, centre, FAR)
    targets = jnp.stack([jnp.where(lat_shift == s, centre, FAR) for s in (-1, 0, 1)], axis=1)
    return jnp.pad(targets, ((0, 0), (0, 0), (0, WINDOW - BLOCK)), constant_values=FAR)


def wave_places(slot_pairs):
    places = slot_pairs.reshape(N_AA, 1, PAIRS) + (jnp.arange(2) * (WAVES // 2))[None, :, None]
    return places.reshape(1, WAVES).astype(jnp.int32)


def local(legendre, spectral, slot_pairs, lat_shift, lon_shift):
    first = lax.axis_index("aa") * PAIRS
    own = lax.axis_index("ba")
    pairs = jnp.stack([slot_pairs[first + own], slot_pairs[first + N_BA + own // 4]])
    rows = lax.all_to_all(pack(legendre, spectral), "ba", 0, 0, tiled=True)
    targets = depart_targets(lat_shift, lon_shift, lax.axis_index("aa") * N_BA)
    pairs, perm, places, targets, bands = lax.optimization_barrier(
        (pairs, regroup_rows(own), wave_places(slot_pairs), targets, edge_bands(targets))
    )
    sums = lax.all_to_all(legendre_sums(pairs, rows), "ba", 0, 0, tiled=True)
    by_row = regroup(perm, sums)
    coefficients = lax.all_to_all(by_row, "aa", 0, 0, tiled=True)
    blocks = synthesize(places, coefficients)
    grid = lax.all_to_all(blocks, "ba", 0, 0, tiled=True)
    ends = jnp.stack([grid[N_BA - 1], grid[0]])
    beside = lax.ppermute(ends, "aa", [(i, (i + 1) % N_AA) for i in range(N_AA)])
    inner = depart_inner(targets, grid)
    return depart_edges(inner, bands, beside, grid)


def solution(mesh):
    placed = (
        P("aa", None, "ba", None, None),
        P("aa", None, None, "ba"),
        P(),
        P("aa", "ba"),
        P("aa", "ba"),
    )
    return jax.shard_map(
        local, mesh=mesh, in_specs=placed, out_specs=P("aa", None, "ba"), check_vma=False
    )
```

```python
import math

import jax
import jax.numpy as jnp
import numpy as np
from jax import lax
from jax.experimental import pallas as pl
from jax.experimental.pallas import tpu as pltpu
from jax.sharding import PartitionSpec as P

WAVES = 1280
NLON = 5120
FL = 64
KPACK = 1281
KTILES = 10
TILES = 7 * KTILES + 1
N_AA = 32
N_BA = 16
PAIRS = 20
HALO = 32
QUARTER = NLON // 4
BLOCK = NLON // N_BA
WINDOW = BLOCK + 2 * HALO
BF16 = jnp.bfloat16
F32 = jnp.float32
NT = (((1,), (1,)), ((), ()))
FAR = -1000.0


def params(mib):
    return pltpu.CompilerParams(vmem_limit_bytes=mib * 1024 * 1024)


def whole(count):
    return [pl.BlockSpec(memory_space=pltpu.VMEM)] * count


def wave_order():
    pairs = np.arange(WAVES // 2)
    return np.concatenate([pairs, WAVES - 1 - pairs])


def window_table():
    starts = np.arange(2)[:, None] * BLOCK - HALO
    lons = (starts + np.arange(WINDOW)[None, :]).reshape(-1)
    phases = wave_order()[:, None] * lons[None, :] % NLON
    angles = phases.astype(np.float32) * np.float32(2.0 * math.pi / NLON)
    factor = np.float32(1.0 / math.sqrt(WAVES))
    table = np.stack([np.cos(angles) * factor, -np.sin(angles) * factor], axis=0)
    return table.astype(np.float32).astype(BF16)


def pack_kernel(rows_ref, values_ref, out_ref, rows_held, values_held, out_held, sems):
    into = []
    for q in range(4):
        four = pl.ds(4 * q, 4)
        into.append(
            [
                pltpu.make_async_copy(rows_ref.at[N_BA + q], rows_held.at[N_BA + q], sems.at[q]),
                pltpu.make_async_copy(values_ref.at[N_BA + q], values_held.at[N_BA + q], sems.at[4 + q]),
                pltpu.make_async_copy(rows_ref.at[four], rows_held.at[four], sems.at[8 + q]),
                pltpu.make_async_copy(values_ref.at[four], values_held.at[four], sems.at[12 + q]),
            ]
        )
        for copy in into[q]:
            copy.start()
    out = []
    lane = lax.broadcasted_iota(jnp.int32, (8, 128), 1)
    for d in range(N_BA):
        q, h = d // 4, d % 4
        if h == 0:
            for copy in into[q]:
                copy.wait()
        last = jnp.zeros((8, 128), F32)
        for g in range(7):
            for k in range(KTILES + 1):
                here = slice(128 * k, min(128 * k + 128, KPACK))
                if g < 4:
                    tile = rows_held[d, 8 * g : 8 * g + 8, here]
                elif g == 4:
                    tile = rows_held[N_BA + q, 8 * h : 8 * h + 8, here]
                else:
                    pair = (d, N_BA + q)[g - 5]
                    tile = values_held[pair, :, :, here].reshape(8, here.stop - here.start)
                if k < KTILES:
                    out_held[d, 7 * k + g] = tile
                else:
                    column = jnp.broadcast_to(tile.astype(F32), (8, 128))
                    last = jnp.where(lane == g, column, last)
        out_held[d, TILES - 1] = last.astype(BF16)
        out.append(pltpu.make_async_copy(out_held.at[d], out_ref.at[d], sems.at[PAIRS + 1 + d]))
        out[-1].start()
    for copy in out:
        copy.wait()


def legendre_kernel(pairs_ref, rows_ref, out_ref):
    column = lax.broadcasted_iota(jnp.int32, (1, 128 * KTILES), 1)
    lane = lax.broadcasted_iota(jnp.int32, (1, 128), 1)
    last = rows_ref[:, TILES - 1]
    for which, (first, count, value) in enumerate(((0, 4, 5), (4, 1, 6))):
        total = N_BA * 8 * count
        left = [
            rows_ref[:, 7 * k + first : 7 * k + first + count].reshape(total, 128)
            for k in range(KTILES)
        ]
        ends = [last * (lane == first + g).astype(F32).astype(BF16) for g in range(count)]
        left.append(jnp.stack(ends, axis=1).reshape(total, 128))
        values = [rows_ref[:, 7 * k + value].reshape(128, 128) for k in range(KTILES)]
        values = jnp.concatenate(values, axis=1)
        end = last.reshape(128, 128)[:, value : value + 1].astype(F32)
        end = jnp.broadcast_to(end, (128, 128)).astype(BF16)
        lower = (column < WAVES - pairs_ref[which]).astype(F32)
        right = jnp.concatenate(
            [
                jnp.concatenate([values * lower.astype(BF16), jnp.zeros_like(end)], axis=1),
                jnp.concatenate([values * (1.0 - lower).astype(BF16), end], axis=1),
            ],
            axis=0,
        )
        left = jnp.concatenate(left, axis=1)
        out = lax.dot_general(left, right, NT, preferred_element_type=F32).astype(BF16)
        out_ref[:, 8 * first : 8 * (first + count), :] = out.reshape(N_BA, 8 * count, 256)


def regroup_rows_kernel(own_ref, out_ref):
    row = iota((WAVES, 1), 0)
    lat = (row // 40 + jnp.where(own_ref[0] == 0, 1, 0)) % N_AA
    pair = row % PAIRS
    shared = (4 * (pair - N_BA) + lat // 8) * 40 + 32 + lat % 8
    source = jnp.where(pair < N_BA, pair * 40 + lat, shared)
    out_ref[...] = ones_where(iota((WAVES, N_BA * 40), 1) == source)


def regroup_kernel(perm_ref, sums_ref, out_ref):
    sums = sums_ref[...].reshape(N_BA * 40, 256)
    both = jnp.dot(perm_ref[...], sums, preferred_element_type=F32)
    first = iota((WAVES, 128), 0) // PAIRS % 2 == 0
    out = jnp.where(first, both[:, :128], both[:, 128:]).astype(BF16)
    out_ref[...] = out.reshape(N_AA, 40, 128)


def iota(shape, dim):
    return lax.broadcasted_iota(jnp.int32, shape, dim)


def ones_where(chosen):
    return chosen.astype(F32).astype(BF16)


def column_kernel(places_ref, out_ref):
    row = jnp.broadcast_to(places_ref[...].astype(F32), (8, WAVES))
    out_ref[...] = jnp.broadcast_to(row.T[:, :1], (WAVES, 128)).astype(jnp.int32)


def synthesis_kernel(places_ref, coef_ref, table_ref, out_ref, left_ref):
    row, lane = iota((128, 128), 0), iota((128, 128), 1)
    fields = ones_where(lane == (row % FL) // 4 * 8 + row // FL * 4 + row % 4)
    chosen = ones_where(iota((WAVES, WAVES), 1) == places_ref[:, :1])
    rows = coef_ref[...].reshape(WAVES, 128)
    turned = lax.dot_general(fields, rows, NT, preferred_element_type=F32).astype(BF16)
    ordered = jnp.dot(turned, chosen, preferred_element_type=F32)
    real, imag = ordered[:FL], ordered[FL:]
    place = iota((1, WAVES), 1)
    wave = jnp.where(place < WAVES // 2, place, WAVES + WAVES // 2 - 1 - place)
    for q in range(4):
        turn = wave * q % 4
        alpha = (turn == 0).astype(F32) - (turn == 2).astype(F32)
        beta = (turn == 1).astype(F32) - (turn == 3).astype(F32)
        here = pl.ds(q * FL, FL)
        left_ref[0, here, :] = (real * alpha - imag * beta).astype(BF16)
        left_ref[1, here, :] = (imag * alpha + real * beta).astype(BF16)
    even = jnp.dot(left_ref[0], table_ref[0], preferred_element_type=F32)
    odd = jnp.dot(left_ref[1], table_ref[1], preferred_element_type=F32)
    ahead, behind = (even + odd).astype(BF16), (even - odd).astype(BF16)
    mirror = ones_where(iota((WINDOW, WINDOW), 0) + iota((WINDOW, WINDOW), 1) == WINDOW)
    for w in range(2):
        lanes = slice(w * WINDOW, (w + 1) * WINDOW)
        back = jnp.dot(behind[:, lanes], mirror, preferred_element_type=F32).astype(BF16)
        for q in range(4):
            here = slice(q * FL, (q + 1) * FL)
            out_ref[4 * q + w] = ahead[here, lanes]
            out_ref[(4 * q + N_BA - 1 - w) % N_BA] = back[here]


def band(target, first, count):
    offset = lax.broadcasted_iota(jnp.int32, (count, 128), 0) + (first - 96)
    distance = jnp.abs(offset.astype(F32).astype(BF16) - target.astype(BF16))
    inner = 0.875 - 0.625 * distance
    outer = jnp.minimum(0.0625 * distance - 0.15625, 0.0)
    return jnp.maximum(inner, outer).astype(BF16)


def clear(bands):
    for held in bands:
        held[...] = jnp.zeros_like(held)


def fill_bands(target_ref, at, bands):
    for t, (part, lanes, last, first) in enumerate(((0, 384, 176, 0), (0, 384, 176, 128), (1, 128, 112, 0))):
        for step in range(3):
            target = target_ref[at, step : step + 1, t * 128 : (t + 1) * 128]
            target = jnp.broadcast_to(target, (last - 16, 128))
            begin = step * lanes + first + 16
            bands[part][begin : begin + last - 16, first : first + 128] = band(target, 16, last - 16)


def multiply_bands(sources, bands, out_ref, to):
    for part, (lane, x, width) in enumerate(((0, 0, 256), (256, 256, 64))):
        left = jnp.concatenate([s[:, lane:] for s in sources], axis=1)
        out = jnp.dot(left, bands[part][...], preferred_element_type=F32).astype(BF16)
        out_ref[to, :, x : x + width] = out[:, :width]


def inner_kernel(target_ref, grid_ref, out_ref, *bands):
    clear(bands)

    @pl.loop(2, N_BA, unroll=14)
    def _(row):
        above = jnp.where(row == N_BA - 1, 0, row + 1)
        sources = [grid_ref.at[row - 1], grid_ref.at[row], grid_ref.at[above]]
        fill_bands(target_ref, row, bands)
        multiply_bands(sources, bands, out_ref, row)


def edge_bands_kernel(target_ref, *bands):
    clear(bands)
    for row in range(2):
        fill_bands(target_ref, row, [held.at[row] for held in bands])


def edge_kernel(inner_ref, wide_ref, narrow_ref, beside_ref, grid_ref, out_ref):
    sources = [beside_ref.at[0], beside_ref.at[1], grid_ref.at[1], grid_ref.at[2]]
    for row in range(2):
        bands = [wide_ref.at[row], narrow_ref.at[row]]
        multiply_bands(sources[row : row + 3], bands, out_ref, row)


def pack(legendre, spectral):
    rows = legendre.reshape(PAIRS, N_AA, KPACK)
    values = spectral.transpose(0, 2, 3, 1)
    anywhere = pl.BlockSpec(memory_space=pl.ANY)
    return pl.pallas_call(
        pack_kernel,
        out_shape=jax.ShapeDtypeStruct((N_BA, TILES, 8, 128), BF16),
        in_specs=[anywhere, anywhere],
        out_specs=anywhere,
        scratch_shapes=[
            pltpu.VMEM((PAIRS, N_AA, KPACK), BF16),
            pltpu.VMEM((PAIRS, 2, 4, KPACK), BF16),
            pltpu.VMEM((N_BA, TILES, 8, 128), BF16),
            pltpu.SemaphoreType.DMA((PAIRS + 1 + N_BA,)),
        ],
        compiler_params=params(59),
        name="pack",
    )(rows, values)


def legendre_sums(pairs, rows):
    return pl.pallas_call(
        legendre_kernel,
        out_shape=jax.ShapeDtypeStruct((N_BA, 40, 256), BF16),
        in_specs=[pl.BlockSpec(memory_space=pltpu.SMEM)] + whole(1),
        out_specs=whole(1)[0],
        compiler_params=params(24),
        name="legendre_sums",
    )(pairs, rows)


def regroup(perm, sums):
    return pl.pallas_call(
        regroup_kernel,
        out_shape=jax.ShapeDtypeStruct((N_AA, 40, 128), BF16),
        in_specs=whole(2),
        out_specs=whole(1)[0],
        compiler_params=params(24),
        name="regroup",
    )(perm, sums)


def regroup_rows(own):
    return pl.pallas_call(
        regroup_rows_kernel,
        out_shape=jax.ShapeDtypeStruct((WAVES, N_BA * 40), BF16),
        in_specs=[pl.BlockSpec(memory_space=pltpu.SMEM)],
        out_specs=whole(1)[0],
        compiler_params=params(8),
        name="regroup_rows",
    )(own.reshape(1).astype(jnp.int32))


def column_places(places):
    return pl.pallas_call(
        column_kernel,
        out_shape=jax.ShapeDtypeStruct((WAVES, 128), jnp.int32),
        in_specs=whole(1),
        out_specs=whole(1)[0],
        compiler_params=params(8),
        name="column_places",
    )(places)


def synthesize(places, coefficients):
    return pl.pallas_call(
        synthesis_kernel,
        out_shape=jax.ShapeDtypeStruct((N_BA, FL, WINDOW), BF16),
        in_specs=whole(3),
        out_specs=whole(1)[0],
        scratch_shapes=[pltpu.VMEM((2, 4 * FL, WAVES), BF16)],
        compiler_params=params(24),
        name="synthesize",
    )(places, coefficients, jnp.asarray(window_table()))


def band_scratch():
    return [pltpu.VMEM((1152, 256), BF16), pltpu.VMEM((384, 128), BF16)]


def depart_inner(targets, grid):
    return pl.pallas_call(
        inner_kernel,
        out_shape=jax.ShapeDtypeStruct((N_BA, FL, BLOCK), BF16),
        in_specs=whole(2),
        out_specs=whole(1)[0],
        scratch_shapes=band_scratch(),
        compiler_params=params(24),
        cost_estimate=pl.CostEstimate(
            flops=2 * 14 * FL * 1920 * 128, bytes_accessed=4000000, transcendentals=0
        ),
        name="depart_inner",
    )(targets, grid)


def edge_bands(targets):
    return pl.pallas_call(
        edge_bands_kernel,
        out_shape=(
            jax.ShapeDtypeStruct((2, 1152, 256), BF16),
            jax.ShapeDtypeStruct((2, 384, 128), BF16),
        ),
        in_specs=whole(1),
        out_specs=tuple(whole(2)),
        compiler_params=params(8),
        name="edge_bands",
    )(targets)


def depart_edges(inner, bands, beside, grid):
    return pl.pallas_call(
        edge_kernel,
        grid=(1,),
        out_shape=jax.ShapeDtypeStruct((N_BA, FL, BLOCK), BF16),
        in_specs=[pl.BlockSpec(memory_space=pl.ANY)] + whole(4),
        out_specs=pl.BlockSpec((2, FL, BLOCK), lambda e: (0, 0, 0)),
        input_output_aliases={0: 0},
        compiler_params=params(24),
        name="depart_edges",
    )(inner, *bands, beside, grid)


def depart_targets(lat_shift, lon_shift, first_row):
    x = jnp.arange(BLOCK, dtype=jnp.int32) % 128
    centre = (x + lon_shift).astype(F32) + (HALO - 1 + 1.5 - 96)
    sources = first_row + jnp.arange(N_BA, dtype=jnp.int32)[:, None] + lat_shift
    inside = jnp.logical_and(sources >= 0, sources < N_AA * N_BA)
    centre = jnp.where(inside, centre, FAR)
    targets = jnp.stack([jnp.where(lat_shift == s, centre, FAR) for s in (-1, 0, 1)], axis=1)
    return jnp.pad(targets, ((0, 0), (0, 0), (0, WINDOW - BLOCK)), constant_values=FAR)


def wave_places(slot_pairs):
    places = slot_pairs.reshape(N_AA, 1, PAIRS) + (jnp.arange(2) * (WAVES // 2))[None, :, None]
    return places.reshape(1, WAVES).astype(jnp.int32)


def local(legendre, spectral, slot_pairs, lat_shift, lon_shift):
    first = lax.axis_index("aa") * PAIRS
    own = lax.axis_index("ba")
    pairs = jnp.stack([slot_pairs[first + own], slot_pairs[first + N_BA + own // 4]])
    rows = lax.all_to_all(pack(legendre, spectral), "ba", 0, 0, tiled=True)
    targets = depart_targets(lat_shift, lon_shift, lax.axis_index("aa") * N_BA)
    pairs, perm, places, targets, bands = lax.optimization_barrier(
        (pairs, regroup_rows(own), column_places(wave_places(slot_pairs)), targets, edge_bands(targets))
    )
    sums = lax.all_to_all(legendre_sums(pairs, rows), "ba", 0, 0, tiled=True)
    by_row = regroup(perm, sums)
    coefficients = lax.all_to_all(by_row, "aa", 0, 0, tiled=True)
    blocks = synthesize(places, coefficients)
    grid = lax.all_to_all(blocks, "ba", 0, 0, tiled=True)
    ends = jnp.stack([grid[N_BA - 1], grid[0]])
    beside = lax.ppermute(ends, "aa", [(i, (i + 1) % N_AA) for i in range(N_AA)])
    inner = depart_inner(targets, grid)
    return depart_edges(inner, bands, beside, grid)


def solution(mesh):
    placed = (
        P("aa", None, "ba", None, None),
        P("aa", None, None, "ba"),
        P(),
        P("aa", "ba"),
        P("aa", "ba"),
    )
    return jax.shard_map(
        local, mesh=mesh, in_specs=placed, out_specs=P("aa", None, "ba"), check_vma=False
    )
```

```python
import math

import jax
import jax.numpy as jnp
import numpy as np
from jax import lax
from jax.experimental import pallas as pl
from jax.experimental.pallas import tpu as pltpu
from jax.sharding import PartitionSpec as P

WAVES = 1280
NLON = 5120
FL = 64
KPACK = 1281
KTILES = 10
TILES = 7 * KTILES + 1
N_AA = 32
N_BA = 16
PAIRS = 20
HALO = 32
QUARTER = NLON // 4
BLOCK = NLON // N_BA
WINDOW = BLOCK + 2 * HALO
BF16 = jnp.bfloat16
F32 = jnp.float32
NT = (((1,), (1,)), ((), ()))
FAR = -1000.0


def params(mib):
    return pltpu.CompilerParams(vmem_limit_bytes=mib * 1024 * 1024)


def whole(count):
    return [pl.BlockSpec(memory_space=pltpu.VMEM)] * count


def wave_order():
    pairs = np.arange(WAVES // 2)
    return np.concatenate([pairs, WAVES - 1 - pairs])


def window_table():
    starts = np.arange(2)[:, None] * BLOCK - HALO
    lons = (starts + np.arange(WINDOW)[None, :]).reshape(-1)
    phases = wave_order()[:, None] * lons[None, :] % NLON
    angles = phases.astype(np.float32) * np.float32(2.0 * math.pi / NLON)
    factor = np.float32(1.0 / math.sqrt(WAVES))
    table = np.stack([np.cos(angles) * factor, -np.sin(angles) * factor], axis=0)
    return table.astype(np.float32).astype(BF16)


def pack_kernel(rows_ref, values_ref, out_ref, rows_held, values_held, out_held, sems):
    into = []
    for q in range(4):
        four = pl.ds(4 * q, 4)
        into.append(
            [
                pltpu.make_async_copy(rows_ref.at[N_BA + q], rows_held.at[N_BA + q], sems.at[q]),
                pltpu.make_async_copy(values_ref.at[N_BA + q], values_held.at[N_BA + q], sems.at[4 + q]),
                pltpu.make_async_copy(rows_ref.at[four], rows_held.at[four], sems.at[8 + q]),
                pltpu.make_async_copy(values_ref.at[four], values_held.at[four], sems.at[12 + q]),
            ]
        )
        for copy in into[q]:
            copy.start()
    out = []
    lane = lax.broadcasted_iota(jnp.int32, (8, 128), 1)
    for d in range(N_BA):
        q, h = d // 4, d % 4
        if h == 0:
            for copy in into[q]:
                copy.wait()
        last = jnp.zeros((8, 128), F32)
        for g in range(7):
            for k in range(KTILES + 1):
                here = slice(128 * k, min(128 * k + 128, KPACK))
                if g < 4:
                    tile = rows_held[d, 8 * g : 8 * g + 8, here]
                elif g == 4:
                    tile = rows_held[N_BA + q, 8 * h : 8 * h + 8, here]
                else:
                    pair = (d, N_BA + q)[g - 5]
                    tile = values_held[pair, :, :, here].reshape(8, here.stop - here.start)
                if k < KTILES:
                    out_held[d, 7 * k + g] = tile
                else:
                    column = jnp.broadcast_to(tile.astype(F32), (8, 128))
                    last = jnp.where(lane == g, column, last)
        out_held[d, TILES - 1] = last.astype(BF16)
        out.append(pltpu.make_async_copy(out_held.at[d], out_ref.at[d], sems.at[PAIRS + 1 + d]))
        out[-1].start()
    for copy in out:
        copy.wait()


def legendre_kernel(pairs_ref, rows_ref, out_ref):
    column = lax.broadcasted_iota(jnp.int32, (1, 128 * KTILES), 1)
    lane = lax.broadcasted_iota(jnp.int32, (1, 128), 1)
    last = rows_ref[:, TILES - 1]
    for which, (first, count, value) in enumerate(((0, 4, 5), (4, 1, 6))):
        total = N_BA * 8 * count
        left = [
            rows_ref[:, 7 * k + first : 7 * k + first + count].reshape(total, 128)
            for k in range(KTILES)
        ]
        ends = [last * (lane == first + g).astype(F32).astype(BF16) for g in range(count)]
        left.append(jnp.stack(ends, axis=1).reshape(total, 128))
        values = [rows_ref[:, 7 * k + value].reshape(128, 128) for k in range(KTILES)]
        values = jnp.concatenate(values, axis=1)
        end = last.reshape(128, 128)[:, value : value + 1].astype(F32)
        end = jnp.broadcast_to(end, (128, 128)).astype(BF16)
        lower = (column < WAVES - pairs_ref[which]).astype(F32)
        right = jnp.concatenate(
            [
                jnp.concatenate([values * lower.astype(BF16), jnp.zeros_like(end)], axis=1),
                jnp.concatenate([values * (1.0 - lower).astype(BF16), end], axis=1),
            ],
            axis=0,
        )
        left = jnp.concatenate(left, axis=1)
        out = lax.dot_general(left, right, NT, preferred_element_type=F32).astype(BF16)
        out_ref[:, 8 * first : 8 * (first + count), :] = out.reshape(N_BA, 8 * count, 256)


def regroup_rows_kernel(own_ref, out_ref):
    row = iota((WAVES, 1), 0)
    lat = (row // 40 + jnp.where(own_ref[0] == 0, 1, 0)) % N_AA
    pair = row % PAIRS
    shared = (4 * (pair - N_BA) + lat // 8) * 40 + 32 + lat % 8
    source = jnp.where(pair < N_BA, pair * 40 + lat, shared)
    out_ref[...] = ones_where(iota((WAVES, N_BA * 40), 1) == source)


def regroup_kernel(perm_ref, sums_ref, out_ref):
    sums = sums_ref[...].reshape(N_BA * 40, 256)
    both = jnp.dot(perm_ref[...], sums, preferred_element_type=F32)
    first = iota((WAVES, 128), 0) // PAIRS % 2 == 0
    out = jnp.where(first, both[:, :128], both[:, 128:]).astype(BF16)
    out_ref[...] = out.reshape(N_AA, 40, 128)


def iota(shape, dim):
    return lax.broadcasted_iota(jnp.int32, shape, dim)


def ones_where(chosen):
    return chosen.astype(F32).astype(BF16)


def column_kernel(places_ref, out_ref):
    row = jnp.broadcast_to(places_ref[...].astype(F32), (8, WAVES))
    out_ref[...] = jnp.broadcast_to(row.T[:, :1], (WAVES, 128)).astype(jnp.int32)


def synthesis_kernel(places_ref, coef_ref, table_ref, out_ref, left_ref):
    row, lane = iota((128, 128), 0), iota((128, 128), 1)
    fields = ones_where(lane == (row % FL) // 4 * 8 + row // FL * 4 + row % 4)
    chosen = ones_where(iota((WAVES, WAVES), 1) == places_ref[:, :1])
    rows = coef_ref[...].reshape(WAVES, 128)
    turned = lax.dot_general(fields, rows, NT, preferred_element_type=F32).astype(BF16)
    ordered = jnp.dot(turned, chosen, preferred_element_type=F32)
    real, imag = ordered[:FL], ordered[FL:]
    place = iota((1, WAVES), 1)
    wave = jnp.where(place < WAVES // 2, place, WAVES + WAVES // 2 - 1 - place)
    alpha = (wave % 4 == 0).astype(F32) - (wave % 4 == 2).astype(F32)
    beta = (wave % 4 == 1).astype(F32) - (wave % 4 == 3).astype(F32)
    half = 1.0 - 2.0 * (wave % 2).astype(F32)
    turns = [(real, imag), (real * alpha - imag * beta, imag * alpha + real * beta)]
    for q in range(2):
        for c in range(2):
            left_ref[c, q * FL : (q + 1) * FL, :] = turns[q][c].astype(BF16)
            left_ref[c, (q + 2) * FL : (q + 3) * FL, :] = (turns[q][c] * half).astype(BF16)
    even = jnp.dot(left_ref[0], table_ref[0], preferred_element_type=F32)
    odd = jnp.dot(left_ref[1], table_ref[1], preferred_element_type=F32)
    ahead, behind = (even + odd).astype(BF16), (even - odd).astype(BF16)
    mirror = ones_where(iota((WINDOW, WINDOW), 0) + iota((WINDOW, WINDOW), 1) == WINDOW)
    for w in range(2):
        lanes = slice(w * WINDOW, (w + 1) * WINDOW)
        back = jnp.dot(behind[:, lanes], mirror, preferred_element_type=F32).astype(BF16)
        for q in range(4):
            here = slice(q * FL, (q + 1) * FL)
            out_ref[4 * q + w] = ahead[here, lanes]
            out_ref[(4 * q + N_BA - 1 - w) % N_BA] = back[here]


def band(target, first, count):
    offset = lax.broadcasted_iota(jnp.int32, (count, 128), 0) + (first - 96)
    distance = jnp.abs(offset.astype(F32).astype(BF16) - target.astype(BF16))
    inner = 0.875 - 0.625 * distance
    outer = jnp.minimum(0.0625 * distance - 0.15625, 0.0)
    return jnp.maximum(inner, outer).astype(BF16)


def clear(bands):
    for held in bands:
        held[...] = jnp.zeros_like(held)


def fill_bands(target_ref, at, bands):
    for t, (part, lanes, last, first) in enumerate(((0, 384, 176, 0), (0, 384, 176, 128), (1, 128, 112, 0))):
        for step in range(3):
            target = target_ref[at, step : step + 1, t * 128 : (t + 1) * 128]
            target = jnp.broadcast_to(target, (last - 16, 128))
            begin = step * lanes + first + 16
            bands[part][begin : begin + last - 16, first : first + 128] = band(target, 16, last - 16)


def multiply_bands(sources, bands, out_ref, to):
    for part, (lane, x, width) in enumerate(((0, 0, 256), (256, 256, 64))):
        left = jnp.concatenate([s[:, lane:] for s in sources], axis=1)
        out = jnp.dot(left, bands[part][...], preferred_element_type=F32).astype(BF16)
        out_ref[to, :, x : x + width] = out[:, :width]


def inner_kernel(target_ref, grid_ref, out_ref, *bands):
    clear(bands)

    @pl.loop(2, N_BA, unroll=14)
    def _(row):
        above = jnp.where(row == N_BA - 1, 0, row + 1)
        sources = [grid_ref.at[row - 1], grid_ref.at[row], grid_ref.at[above]]
        fill_bands(target_ref, row, bands)
        multiply_bands(sources, bands, out_ref, row)


def edge_bands_kernel(target_ref, *bands):
    clear(bands)
    for row in range(2):
        fill_bands(target_ref, row, [held.at[row] for held in bands])


def edge_kernel(inner_ref, wide_ref, narrow_ref, beside_ref, grid_ref, out_ref):
    sources = [beside_ref.at[0], beside_ref.at[1], grid_ref.at[1], grid_ref.at[2]]
    for row in range(2):
        bands = [wide_ref.at[row], narrow_ref.at[row]]
        multiply_bands(sources[row : row + 3], bands, out_ref, row)


def pack(legendre, spectral):
    rows = legendre.reshape(PAIRS, N_AA, KPACK)
    values = spectral.transpose(0, 2, 3, 1)
    anywhere = pl.BlockSpec(memory_space=pl.ANY)
    return pl.pallas_call(
        pack_kernel,
        out_shape=jax.ShapeDtypeStruct((N_BA, TILES, 8, 128), BF16),
        in_specs=[anywhere, anywhere],
        out_specs=anywhere,
        scratch_shapes=[
            pltpu.VMEM((PAIRS, N_AA, KPACK), BF16),
            pltpu.VMEM((PAIRS, 2, 4, KPACK), BF16),
            pltpu.VMEM((N_BA, TILES, 8, 128), BF16),
            pltpu.SemaphoreType.DMA((PAIRS + 1 + N_BA,)),
        ],
        compiler_params=params(59),
        name="pack",
    )(rows, values)


def legendre_sums(pairs, rows):
    return pl.pallas_call(
        legendre_kernel,
        out_shape=jax.ShapeDtypeStruct((N_BA, 40, 256), BF16),
        in_specs=[pl.BlockSpec(memory_space=pltpu.SMEM)] + whole(1),
        out_specs=whole(1)[0],
        compiler_params=params(24),
        name="legendre_sums",
    )(pairs, rows)


def regroup(perm, sums):
    return pl.pallas_call(
        regroup_kernel,
        out_shape=jax.ShapeDtypeStruct((N_AA, 40, 128), BF16),
        in_specs=whole(2),
        out_specs=whole(1)[0],
        compiler_params=params(24),
        name="regroup",
    )(perm, sums)


def regroup_rows(own):
    return pl.pallas_call(
        regroup_rows_kernel,
        out_shape=jax.ShapeDtypeStruct((WAVES, N_BA * 40), BF16),
        in_specs=[pl.BlockSpec(memory_space=pltpu.SMEM)],
        out_specs=whole(1)[0],
        compiler_params=params(8),
        name="regroup_rows",
    )(own.reshape(1).astype(jnp.int32))


def column_places(places):
    return pl.pallas_call(
        column_kernel,
        out_shape=jax.ShapeDtypeStruct((WAVES, 128), jnp.int32),
        in_specs=whole(1),
        out_specs=whole(1)[0],
        compiler_params=params(8),
        name="column_places",
    )(places)


def synthesize(places, coefficients):
    return pl.pallas_call(
        synthesis_kernel,
        out_shape=jax.ShapeDtypeStruct((N_BA, FL, WINDOW), BF16),
        in_specs=whole(3),
        out_specs=whole(1)[0],
        scratch_shapes=[pltpu.VMEM((2, 4 * FL, WAVES), BF16)],
        compiler_params=params(24),
        name="synthesize",
    )(places, coefficients, jnp.asarray(window_table()))


def band_scratch():
    return [pltpu.VMEM((1152, 256), BF16), pltpu.VMEM((384, 128), BF16)]


def depart_inner(targets, grid):
    return pl.pallas_call(
        inner_kernel,
        out_shape=jax.ShapeDtypeStruct((N_BA, FL, BLOCK), BF16),
        in_specs=whole(2),
        out_specs=whole(1)[0],
        scratch_shapes=band_scratch(),
        compiler_params=params(24),
        cost_estimate=pl.CostEstimate(
            flops=2 * 14 * FL * 1920 * 128, bytes_accessed=4000000, transcendentals=0
        ),
        name="depart_inner",
    )(targets, grid)


def edge_bands(targets):
    return pl.pallas_call(
        edge_bands_kernel,
        out_shape=(
            jax.ShapeDtypeStruct((2, 1152, 256), BF16),
            jax.ShapeDtypeStruct((2, 384, 128), BF16),
        ),
        in_specs=whole(1),
        out_specs=tuple(whole(2)),
        compiler_params=params(8),
        name="edge_bands",
    )(targets)


def depart_edges(inner, bands, beside, grid):
    return pl.pallas_call(
        edge_kernel,
        grid=(1,),
        out_shape=jax.ShapeDtypeStruct((N_BA, FL, BLOCK), BF16),
        in_specs=[pl.BlockSpec(memory_space=pl.ANY)] + whole(4),
        out_specs=pl.BlockSpec((2, FL, BLOCK), lambda e: (0, 0, 0)),
        input_output_aliases={0: 0},
        compiler_params=params(24),
        name="depart_edges",
    )(inner, *bands, beside, grid)


def depart_targets(lat_shift, lon_shift, first_row):
    x = jnp.arange(BLOCK, dtype=jnp.int32) % 128
    centre = (x + lon_shift).astype(F32) + (HALO - 1 + 1.5 - 96)
    sources = first_row + jnp.arange(N_BA, dtype=jnp.int32)[:, None] + lat_shift
    inside = jnp.logical_and(sources >= 0, sources < N_AA * N_BA)
    centre = jnp.where(inside, centre, FAR)
    targets = jnp.stack([jnp.where(lat_shift == s, centre, FAR) for s in (-1, 0, 1)], axis=1)
    return jnp.pad(targets, ((0, 0), (0, 0), (0, WINDOW - BLOCK)), constant_values=FAR)


def wave_places(slot_pairs):
    places = slot_pairs.reshape(N_AA, 1, PAIRS) + (jnp.arange(2) * (WAVES // 2))[None, :, None]
    return places.reshape(1, WAVES).astype(jnp.int32)


def local(legendre, spectral, slot_pairs, lat_shift, lon_shift):
    first = lax.axis_index("aa") * PAIRS
    own = lax.axis_index("ba")
    pairs = jnp.stack([slot_pairs[first + own], slot_pairs[first + N_BA + own // 4]])
    rows = lax.all_to_all(pack(legendre, spectral), "ba", 0, 0, tiled=True)
    targets = depart_targets(lat_shift, lon_shift, lax.axis_index("aa") * N_BA)
    pairs, perm, places, targets, bands = lax.optimization_barrier(
        (pairs, regroup_rows(own), column_places(wave_places(slot_pairs)), targets, edge_bands(targets))
    )
    sums = lax.all_to_all(legendre_sums(pairs, rows), "ba", 0, 0, tiled=True)
    by_row = regroup(perm, sums)
    coefficients = lax.all_to_all(by_row, "aa", 0, 0, tiled=True)
    blocks = synthesize(places, coefficients)
    grid = lax.all_to_all(blocks, "ba", 0, 0, tiled=True)
    ends = jnp.stack([grid[N_BA - 1], grid[0]])
    beside = lax.ppermute(ends, "aa", [(i, (i + 1) % N_AA) for i in range(N_AA)])
    inner = depart_inner(targets, grid)
    return depart_edges(inner, bands, beside, grid)


def solution(mesh):
    placed = (
        P("aa", None, "ba", None, None),
        P("aa", None, None, "ba"),
        P(),
        P("aa", "ba"),
        P("aa", "ba"),
    )
    return jax.shard_map(
        local, mesh=mesh, in_specs=placed, out_specs=P("aa", None, "ba"), check_vma=False
    )
```
